128 devices in a mesh: role: 2 (over core), dp: 8 (over y, x_lo), tensor: 8 (over z, x_hi).
Axes of the slice: x: 4 (x_hi: 2, x_lo: 2; x = x_hi * 2 + x_lo), y: 4, z: 4, core: 2. Of those that a mesh axis runs over, the one named last changes fastest.
Arguments:
- teacher_in: bfloat16 [2, 2048, 16384], P(None, 'dp', ('role', 'tensor')), may hold values from -16 to 16
- teacher_weight: bfloat16 [16384, 8192], P(('role', 'tensor')), may hold values from -0.046875 to 0.046875
- student_in: bfloat16 [4096, 8192], P(('role', 'dp')), may hold values from -6 to 6
- student_weight: bfloat16 [8192, 4096], P(('role', 'dp'), 'tensor'), may hold values from -0.0625 to 0.0625
- projector: bfloat16 [4096, 8192], P('tensor', ('role', 'dp')), may hold values from -0.09375 to 0.09375
Outputs:
- grad_weight: float32 [8192, 4096], P(('role', 'dp'), 'tensor')
- loss: float32 [], replicated
The draws below stay inside these ranges and needn't reach their ends.
All inputs are finite; a program needn't handle non-finite values.
Results may differ from the reference program's by a relative error of at most 0.015.
Values may be sent and summed in bfloat16 or wider, within the bound.
No kernel may reach another device: no remote copies, remote signals or barrier semaphores. Data moves between devices by JAX's collectives and lax.ppermute only.
A program may use at most 192 MiB of HBM per device.

```python
import jax
import jax.numpy as jnp
from jax import lax

DT = 16384
DS = 8192
TW = 8192
SH = 4096
TOKENS = 4096
N_ROLE = 2
N_TENSOR = 8


def draw_teacher_in(key, part):
    key = jax.random.fold_in(key, 7)
    noise_key = jax.random.fold_in(key, 0)
    shape = (N_ROLE, TOKENS // N_ROLE, DT)
    where = (jnp.arange(TOKENS, dtype=jnp.float32) / TOKENS).reshape(N_ROLE, TOKENS // N_ROLE, 1)
    base = jnp.clip(jax.random.normal(noise_key, shape, jnp.float32), -6.0, 6.0)
    rise = 0.5 * jnp.exp(1.38 * where)
    return (base * rise).astype(jnp.bfloat16)


def levels(stream_key, extent, cuts, low, high):
    factor_of, own = 1.0, jax.random.fold_in(stream_key, 6)
    for dim, parts in cuts:
        heights = jnp.exp(jax.random.uniform(jax.random.fold_in(own, dim), (parts,), jnp.float32, low / len(cuts), high / len(cuts)))
        factor_of = factor_of * jnp.repeat(heights, extent[dim] // parts).reshape([-1 if axis == dim else 1 for axis in range(len(extent))])
    return factor_of


def noise(own_key, shape, scale, bound, shards=(), held_as=jnp.bfloat16):
    loudness = levels(own_key, shape, shards, -0.22, 0.18) if shards else 1.0
    array = jax.random.normal(own_key, shape, jnp.float32) * scale * loudness
    return jnp.minimum(jnp.maximum(array, -bound), bound).astype(held_as)


def setup_inputs(seed: int = 0) -> dict:
    arg_keys = jax.random.split(jax.random.key(seed), 6)
    return {
        "teacher_in": draw_teacher_in(jax.random.fold_in(arg_keys[5], 71), 0),
        "teacher_weight": noise(arg_keys[1], (DT, TW), DT ** -0.5, 0.046875, ((0, 16),)),
        "student_in": noise(arg_keys[2], (TOKENS, DS), 1.0, 6.0, ((0, 16),)),
        "student_weight": noise(arg_keys[3], (DS, SH), DS ** -0.5, 0.0625, ((0, 16), (1, 8))),
        "projector": noise(arg_keys[4], (SH, TW), SH ** -0.5, 0.09375, ((0, 8), (1, 16))),
    }


def blocked_sum(left, right, groups):
    width = left.shape[1] // groups
    total = jnp.zeros((left.shape[0], right.shape[1]), jnp.float32)
    for group in range(groups):
        term = jnp.dot(left[:, group * width:(group + 1) * width], right[group * width:(group + 1) * width, :], preferred_element_type=jnp.float32)
        rounded = lax.optimization_barrier(term.astype(jnp.bfloat16))
        total = total + rounded.astype(jnp.float32)
    return total

def reference(teacher_in, teacher_weight, student_in, student_weight, projector):
    teacher_rows = teacher_in.reshape(TOKENS, DT)
    teacher_hidden = jnp.dot(teacher_rows, teacher_weight, preferred_element_type=jnp.float32)
    pre = jnp.dot(student_in, student_weight, preferred_element_type=jnp.float32)
    hidden = jax.nn.silu(pre).astype(jnp.bfloat16)
    projection = blocked_sum(hidden, projector, N_TENSOR)
    difference = projection - teacher_hidden
    loss = jnp.sum(difference * difference) / (2.0 * TOKENS * TW)
    residual = difference.astype(jnp.bfloat16)
    back = lax.dot_general(residual, projector, (((1,), (1,)), ((), ())), preferred_element_type=jnp.float32)
    sigma = jax.nn.sigmoid(pre)
    delta = (back * sigma * (1.0 + pre * (1.0 - sigma))).astype(jnp.bfloat16)
    grad_weight = lax.dot_general(student_in, delta, (((0,), (0,)), ((), ())), preferred_element_type=jnp.float32)
    return (grad_weight / jnp.sqrt(jnp.float32(TOKENS)), loss)
```

```python
import jax
import jax.numpy as jnp
from jax import lax
from jax.sharding import PartitionSpec as P

BF16 = jnp.bfloat16
F32 = jnp.float32
OFFSETS = ((0, 0), (0, 1), (1, 0), (-1, 0), (2, 0), (1, 1), (-1, 1), (2, 1))


def shift(value, axis, k, e):
    perm = [(i, ((i // 2 + k) % 4) * 2 + ((i % 2) ^ e)) for i in range(8)]
    return lax.ppermute(value, axis, perm)


def flip(value, axis, bit):
    return lax.ppermute(value, axis, [(i, i ^ bit) for i in range(lax.axis_size(axis))])


def sources(axis):
    me = lax.axis_index(axis)
    return [((me // 2 - k + 4) % 4) * 2 + (me % 2 + e) % 2 for k, e in OFFSETS]


def gather(block, axis):
    half = block.shape[0] // 2
    other = shift(block, axis, 0, 1)
    before = shift(block, axis, 1, 0)
    after = shift(block, axis, -1, 0)
    far = jnp.concatenate(
        [shift(before[:half], axis, 1, 0), shift(after[half:], axis, -1, 0)], axis=0
    )
    other_before = shift(other, axis, 1, 0)
    other_after = shift(other, axis, -1, 0)
    other_far = shift(far, axis, 0, 1)
    return [block, other, before, after, far, other_before, other_after, other_far]


def scatter_ring_first(blocks, axis):
    by = dict(zip(OFFSETS, blocks))
    near, cross = by[0, 0], by[0, 1]
    rows = near.shape[0]
    for k in (1, -1, 2):
        pair = jnp.concatenate([by[k, 0], by[k, 1]], axis=0).astype(BF16)
        got = shift(pair, axis, -k, 0).astype(F32)
        near = near + got[:rows]
        cross = cross + got[rows:]
    return near + shift(cross.astype(BF16), axis, 0, 1).astype(F32)


def scatter_pair_first(blocks, axis):
    by = dict(zip(OFFSETS, blocks))
    rows = blocks[0].shape[0]
    ring = (1, -1, 2, 0)
    sums = {}
    for k in ring:
        sums[k] = by[k, 0] + shift(by[k, 1].astype(BF16), axis, 0, 1).astype(F32)
    total = sums[0]
    for k in (1, -1, 2):
        total = total + shift(sums[k].astype(BF16), axis, -k, 0).astype(F32)
    return total


def dot(a, b, dims=((1,), (0,))):
    return lax.dot_general(a, b, (dims, ((), ())), preferred_element_type=F32)


def shards(teacher_in, teacher_weight, student_in, student_weight, projector):
    role = lax.axis_index("role")
    n_role = lax.axis_size("role")
    n_model = lax.axis_size("tensor")
    total_rows = student_in.shape[0] * n_role * lax.axis_size("dp")
    out_width = teacher_weight.shape[1]
    rows = 2 * student_in.shape[0]
    part = rows // n_model
    feat = student_weight.shape[0]
    cols = projector.shape[1]
    wide = feat * 8
    half = out_width // 2
    feat_from = sources("dp")
    row_from = sources("tensor")

    w_blocks = gather(student_weight, "dp")
    p_blocks = gather(projector, "dp")

    mine = lax.dynamic_slice_in_dim(student_in, role * wide, wide, axis=1)
    theirs = lax.dynamic_slice_in_dim(student_in, (1 - role) * wide, wide, axis=1)
    theirs = flip(theirs, "role", 1)
    both = jnp.where(
        role == 0, jnp.concatenate([mine, theirs], 0), jnp.concatenate([theirs, mine], 0)
    )
    both = jnp.concatenate(
        [lax.dynamic_slice_in_dim(both, s * part, part, axis=0) for s in row_from], axis=0
    )
    both = jnp.concatenate(
        [lax.dynamic_slice_in_dim(both, s * feat, feat, axis=1) for s in feat_from], axis=1
    )

    teacher_rows = teacher_in.reshape(rows, teacher_in.shape[2])
    teacher_rows = jnp.concatenate(
        [lax.dynamic_slice_in_dim(teacher_rows, s * part, part, axis=0) for s in row_from], axis=0
    )
    away = dot(teacher_rows, lax.dynamic_slice_in_dim(teacher_weight, (1 - role) * half, half, axis=1))
    away = flip(away.astype(BF16), "role", 1)
    teacher = dot(teacher_rows, lax.dynamic_slice_in_dim(teacher_weight, role * half, half, axis=1))
    teacher = teacher + away.astype(F32)

    pre = dot(both, jnp.concatenate(w_blocks, axis=0))
    pre = pre + flip(pre, "role", 1)
    sigma = jax.nn.sigmoid(pre)
    hidden = (pre * sigma).astype(BF16)

    square = jnp.zeros((), F32)
    residual_groups, p_groups = [], []
    for group in (range(0, 4), range(4, 8)):
        p_group = jnp.concatenate([p_blocks[j] for j in group], axis=1)
        t_group = jnp.concatenate(
            [lax.dynamic_slice_in_dim(teacher, feat_from[j] * cols, cols, axis=1) for j in group], axis=1
        )
        partial = dot(hidden, p_group) - t_group
        partial = partial.astype(BF16)
        difference = scatter_ring_first(
            [partial[i * part : (i + 1) * part].astype(F32) for i in range(8)], "tensor"
        )
        square = square + jnp.sum(difference * difference)
        residual_groups.append(jnp.concatenate(gather(lax.optimization_barrier(difference.astype(BF16)), "tensor"), axis=0))
        p_groups.append(p_group)

    for axis, bit in (("role", 1), ("tensor", 1), ("tensor", 2), ("tensor", 4), ("dp", 1), ("dp", 2), ("dp", 4)):
        square = square + flip(square, axis, bit)
    loss = square / (2.0 * total_rows * out_width)

    back = sum(dot(r, p, ((1,), (1,))) for r, p in zip(residual_groups, p_groups))
    back = back + flip(back, "role", 1)
    delta = (back * sigma * (1.0 + pre * (1.0 - sigma))).astype(BF16)

    grad = dot(both, delta, ((0,), (0,))).astype(BF16)
    mid = feat // 2
    blocks = [grad[j * feat : (j + 1) * feat].astype(F32) for j in range(8)]
    left = scatter_pair_first([b[:mid] for b in blocks], "dp")
    right = scatter_ring_first([b[mid:] for b in blocks], "dp")
    grad_weight = jnp.concatenate([left, right], axis=0)
    return (grad_weight / jnp.sqrt(jnp.float32(total_rows)), loss)


def solution(mesh):
    in_specs = (
        P(None, "dp", ("role", "tensor")),
        P(("role", "tensor"), None),
        P(("role", "dp"), None),
        P(("role", "dp"), "tensor"),
        P("tensor", ("role", "dp")),
    )
    out_specs = (P(("role", "dp"), "tensor"), P())
    return jax.shard_map(shards, mesh=mesh, in_specs=in_specs, out_specs=out_specs, check_vma=False)
```

```python
import jax
import jax.numpy as jnp
from jax import lax
from jax.sharding import PartitionSpec as P

BF16 = jnp.bfloat16
F32 = jnp.float32
NOTE = 16
OFFSETS = ((0, 0), (0, 1), (1, 0), (-1, 0), (2, 0), (1, 1), (-1, 1), (2, 1))


def shift(value, axis, k, e):
    perm = [(i, ((i // 2 + k) % 4) * 2 + ((i % 2) ^ e)) for i in range(8)]
    return lax.ppermute(value, axis, perm)


def flip(value):
    return lax.ppermute(value, "role", [(0, 1), (1, 0)])


def sources(axis):
    me = lax.axis_index(axis)
    return [((((me >> 1) - k) & 3) << 1) | ((me & 1) ^ e) for k, e in OFFSETS]


def after(value, *others):
    return lax.optimization_barrier((value, *others))[0]


def gather_start(block, axis):
    return [shift(block, axis, 0, 1), shift(block, axis, 1, 0), shift(block, axis, -1, 0)]


def gather_middle(block, first, axis):
    other, before, nxt = first
    half = block.shape[0] // 2
    up = shift(jnp.concatenate([other, before[:half]], axis=0), axis, 1, 0)
    down = shift(jnp.concatenate([other, nxt[half:]], axis=0), axis, -1, 0)
    return [up, down]


def gather_end(block, first, middle, axis, by_pair):
    other, before, nxt = first
    up, down = middle
    rows = block.shape[0]
    half = rows // 2
    far = jnp.concatenate([up[rows:], down[rows:]], axis=0)
    if by_pair:
        other_far = shift(far, axis, 0, 1)
    else:
        other_far = jnp.concatenate(
            [shift(up[:half], axis, 1, 0), shift(down[half:rows], axis, -1, 0)], axis=0
        )
    return [block, other, before, nxt, far, up[:rows], down[:rows], other_far]


def place(blocks, at, dim):
    size = blocks[0].shape[dim]
    shape = list(blocks[0].shape)
    shape[dim] = 8 * size
    out = jnp.zeros(shape, blocks[0].dtype)
    for block, s in zip(blocks, at):
        out = lax.dynamic_update_slice_in_dim(out, block, s * size, axis=dim)
    return out


def ring_pair(by, k, axis):
    pair = jnp.concatenate([by[k, 0], by[k, 1]], axis=0).astype(BF16)
    return shift(pair, axis, -k, 0)


def ring_end(by, got, axis):
    rows = by[0, 0].shape[0]
    near, cross = by[0, 0].astype(F32), by[0, 1].astype(F32)
    for g in got:
        near = near + g[:rows].astype(F32)
        cross = cross + g[rows:].astype(F32)
    return near + shift(cross.astype(BF16), axis, 0, 1).astype(F32)


def scatter_ring_first(blocks, axis):
    by = dict(zip(OFFSETS, blocks))
    return ring_end(by, [ring_pair(by, k, axis) for k in (1, -1, 2)], axis)


def pack(scalar, width):
    terms = []
    for _ in range(3):
        term = lax.reduce_precision(scalar, 8, 7)
        terms.append(jnp.full((NOTE, width // 4), term).astype(BF16))
        scalar = scalar - term
    return jnp.concatenate(terms + [jnp.zeros((NOTE, width // 4), BF16)], axis=1)


def unpack(note):
    quarter = note.shape[-1] // 4
    return sum(note[..., 0, i * quarter].astype(F32) for i in range(3))


def scatter_pair_first(blocks, axis, scalar):
    by = dict(zip(OFFSETS, blocks))
    rows, width = blocks[0].shape
    ring = (1, -1, 2, 0)
    got = jnp.concatenate([by[k, 1] for k in ring] + [pack(scalar, width)], axis=0).astype(BF16)
    got = shift(got, axis, 0, 1)
    sums = {
        k: by[k, 0].astype(F32) + got[i * rows : (i + 1) * rows].astype(F32)
        for i, k in enumerate(ring)
    }
    scalar = scalar + unpack(got[4 * rows :])
    note = pack(scalar, width)
    total, scalars = sums[0], {0: scalar}
    for k in (1, -1, 2):
        got = shift(jnp.concatenate([sums[k].astype(BF16), note], axis=0), axis, -k, 0)
        total = total + got[:rows].astype(F32)
        scalars[k] = unpack(got[rows:])
    return total, (scalars[0] + scalars[2]) + (scalars[1] + scalars[-1])


def dot(a, b, dims=((1,), (0,))):
    return lax.dot_general(a, b, (dims, ((), ())), preferred_element_type=F32)


def shards(teacher_in, teacher_weight, student_in, student_weight, projector):
    role = lax.axis_index("role")
    n_tensor = lax.axis_size("tensor")
    own_rows = student_in.shape[0]
    rows = 2 * own_rows
    total_rows = rows * lax.axis_size("dp")
    out_width = teacher_weight.shape[1]
    half = out_width // 2
    feat, hid = student_weight.shape
    wide = feat * 8
    cols = projector.shape[1]
    feat_from = sources("dp")
    model_from = sources("tensor")

    swap = [(d * 8 + t, t * 8 + d) for d in range(8) for t in range(8)]

    teacher_rows = teacher_in.reshape(rows, teacher_in.shape[2])
    away = dot(teacher_rows, lax.dynamic_slice_in_dim(teacher_weight, (1 - role) * half, half, axis=1))
    away = flip(away.astype(BF16))
    teacher = dot(teacher_rows, lax.dynamic_slice_in_dim(teacher_weight, role * half, half, axis=1))
    teacher = teacher + away.astype(F32)
    teacher = [lax.dynamic_slice_in_dim(teacher, s * cols, cols, axis=1) for s in model_from]

    w_first = gather_start(student_weight, "dp")
    w_first = lax.optimization_barrier((*w_first, away))[:3]
    w_middle = gather_middle(student_weight, w_first, "dp")
    p_block = lax.ppermute(after(projector, w_first[0]), ("dp", "tensor"), swap)
    *w_middle, p_block = lax.optimization_barrier((*w_middle, p_block))
    weight = gather_end(student_weight, w_first, w_middle, "dp", False)
    weight = place(weight, feat_from, 0)

    p_first = gather_start(after(p_block, *w_middle), "dp")
    teacher = dict(zip(OFFSETS, teacher))
    t_got = [ring_pair(teacher, k, "tensor") for k in (1, -1, 2)]

    mine = lax.dynamic_slice_in_dim(student_in, role * wide, wide, axis=1)
    theirs = flip(lax.dynamic_slice_in_dim(student_in, (1 - role) * wide, wide, axis=1))
    student = jnp.concatenate([mine, theirs], axis=0)

    pre = dot(student, weight)
    pre = pre[:own_rows] + flip(pre[own_rows:])
    sigma = jax.nn.sigmoid(pre)
    hidden = (pre * sigma).astype(BF16)
    hidden, *p_first, t_got[0], t_got[1] = lax.optimization_barrier((hidden, *p_first, t_got[0], t_got[1]))

    p_middle = gather_middle(p_block, p_first, "dp")
    h_first = gather_start(hidden, "tensor")
    h_middle = gather_middle(hidden, h_first, "tensor")
    h_middle[0], *p_middle, t_got[2] = lax.optimization_barrier((h_middle[0], *p_middle, t_got[2]))
    projector = place(gather_end(p_block, p_first, p_middle, "dp", True), feat_from, 0)
    hidden = place(gather_end(hidden, h_first, h_middle, "tensor", True), model_from, 1)
    hidden_other = flip(hidden)
    teacher = ring_end(teacher, t_got, "tensor")

    teacher_own = lax.dynamic_slice_in_dim(teacher, role * own_rows, own_rows, axis=0)
    teacher_other = lax.dynamic_slice_in_dim(teacher, (1 - role) * own_rows, own_rows, axis=0)
    difference = dot(hidden, projector) - teacher_own
    difference_other = dot(hidden_other, projector) - teacher_other
    square = jnp.sum(difference * difference) + jnp.sum(difference_other * difference_other)
    square = square + flip(square)

    back_other = dot(difference_other.astype(BF16), projector, ((1,), (1,)))
    back = dot(difference.astype(BF16), projector, ((1,), (1,))) + flip(back_other.astype(BF16)).astype(F32)
    back = back.astype(BF16)
    note = pack(square, hid)
    back = jnp.concatenate(
        [x for i in range(n_tensor) for x in (back[:, i * hid : (i + 1) * hid], note)], axis=0
    )
    back = lax.all_to_all(back, "tensor", 0, 0, tiled=True)
    back = back.reshape(n_tensor, own_rows + NOTE, hid)
    square = jnp.sum(unpack(back[:, own_rows:]))
    back = jnp.sum(back[:, :own_rows].astype(F32), axis=0)

    delta = (back * sigma * (1.0 + pre * (1.0 - sigma))).astype(BF16)
    delta = jnp.concatenate([delta, flip(delta)], axis=0)

    grad = dot(student, delta, ((0,), (0,))).astype(BF16)
    blocks = [lax.dynamic_slice_in_dim(grad, s * feat, feat, axis=0) for s in feat_from]
    mid = feat // 2
    first, square = scatter_pair_first([b[:mid] for b in blocks], "dp", square)
    second = scatter_ring_first([b[mid:] for b in blocks], "dp")
    loss = square / (2.0 * total_rows * out_width)
    grad_weight = jnp.concatenate([first, second], axis=0)
    return (grad_weight / jnp.sqrt(jnp.float32(total_rows)), loss)


def solution(mesh):
    in_specs = (
        P(None, "dp", ("role", "tensor")),
        P(("role", "tensor"), None),
        P(("role", "dp"), None),
        P(("role", "dp"), "tensor"),
        P("tensor", ("role", "dp")),
    )
    out_specs = (P(("role", "dp"), "tensor"), P())
    return jax.shard_map(shards, mesh=mesh, in_specs=in_specs, out_specs=out_specs, check_vma=False)
```

```python
import jax
import jax.numpy as jnp
from jax import lax
from jax.experimental import pallas as pl
from jax.experimental.pallas import tpu as pltpu
from jax.sharding import PartitionSpec as P

BF16 = jnp.bfloat16
F32 = jnp.float32
NOTE = 16
OFFSETS = ((0, 0), (0, 1), (1, 0), (-1, 0), (2, 0), (1, 1), (-1, 1), (2, 1))


def shift(value, axis, k, e):
    perm = [(i, ((i // 2 + k) % 4) * 2 + ((i % 2) ^ e)) for i in range(8)]
    return lax.ppermute(value, axis, perm)


def flip(value):
    return lax.ppermute(value, "role", [(0, 1), (1, 0)])


def sources(axis):
    me = lax.axis_index(axis)
    return [((((me >> 1) - k) & 3) << 1) | ((me & 1) ^ e) for k, e in OFFSETS]


def after(value, *others):
    return lax.optimization_barrier((value, *others))[0]


def gather_start(block, axis):
    return [shift(block, axis, 0, 1), shift(block, axis, 1, 0), shift(block, axis, -1, 0)]


def gather_middle(block, first, axis):
    other, before, nxt = first
    half = block.shape[0] // 2
    up = shift(jnp.concatenate([other, before[:half]], axis=0), axis, 1, 0)
    down = shift(jnp.concatenate([other, nxt[half:]], axis=0), axis, -1, 0)
    return [up, down]


def gather_end(block, first, middle, axis):
    other, before, nxt = first
    up, down = middle
    rows = block.shape[0]
    far = jnp.concatenate([up[rows:], down[rows:]], axis=0)
    other_far = shift(far, axis, 0, 1)
    return [block, other, before, nxt, far, up[:rows], down[:rows], other_far]


def place(blocks, at, dim):
    size = blocks[0].shape[dim]
    shape = list(blocks[0].shape)
    shape[dim] = 8 * size
    out = jnp.zeros(shape, blocks[0].dtype)
    for block, s in zip(blocks, at):
        out = lax.dynamic_update_slice_in_dim(out, block, s * size, axis=dim)
    return out


def ring_pair(by, k, axis):
    pair = jnp.concatenate([by[k, 0], by[k, 1]], axis=0).astype(BF16)
    return shift(pair, axis, -k, 0)


def ring_end(by, got, axis):
    rows = by[0, 0].shape[0]
    near, cross = by[0, 0].astype(F32), by[0, 1].astype(F32)
    for g in got:
        near = near + g[:rows].astype(F32)
        cross = cross + g[rows:].astype(F32)
    return near + shift(cross.astype(BF16), axis, 0, 1).astype(F32)


def dot(a, b, dims=((1,), (0,))):
    return lax.dot_general(a, b, (dims, ((), ())), preferred_element_type=F32)


def split_note(value, width):
    value = jnp.broadcast_to(value, (1, width)).astype(F32)
    row = lax.broadcasted_iota(jnp.int32, (NOTE, width), 0)
    high = lax.reduce_precision(value, 8, 7)
    middle = lax.reduce_precision(value - high, 8, 7)
    low = value - high - middle
    note = jnp.where(row == 0, high, jnp.where(row == 1, middle, jnp.where(row == 2, low, 0.0)))
    return note.astype(BF16)


def join_note(note):
    return jnp.sum(note.astype(F32), axis=0, keepdims=True)


def project_kernel(hidden, projector, teacher, out, low, high, square):
    step, block = pl.program_id(0), pl.program_id(1)
    n, width = out.shape[0] - NOTE, out.shape[1]

    @pl.when((step == 0) & (block == 0))
    def _():
        low[...] = jnp.zeros_like(low)
        high[...] = jnp.zeros_like(high)

    @pl.when(step == 0)
    def _():
        low[...] += jnp.dot(hidden[...], projector[0], preferred_element_type=F32)
        high[...] += jnp.dot(hidden[...], projector[1], preferred_element_type=F32)

    @pl.when((step == 1) & (block == 0))
    def _():
        low[...] -= teacher[:, :width]
        high[...] -= teacher[:, width:]
        square[...] = jnp.broadcast_to(
            jnp.sum(low[...] * low[...] + high[...] * high[...], keepdims=True), square.shape
        )

    @pl.when(step == 1)
    def _():
        dims = (((1,), (1,)), ((), ()))
        back = lax.dot_general(low[...].astype(BF16), projector[0], dims, preferred_element_type=F32)
        back += lax.dot_general(high[...].astype(BF16), projector[1], dims, preferred_element_type=F32)
        out[:n] = back.astype(BF16)
        value = square[:1]
        row = lax.broadcasted_iota(jnp.int32, (NOTE, width), 0)
        top = value.astype(BF16).astype(F32)
        middle = (value - top).astype(BF16).astype(F32)
        bottom = value - top - middle
        note = jnp.where(row == 0, top, jnp.where(row == 1, middle, jnp.where(row == 2, bottom, 0.0)))
        out[n:] = note.astype(BF16)


def project(hidden, projector, teacher):
    rows, total = hidden.shape
    blocks = projector.shape[1]
    width = projector.shape[3]
    size = total // blocks
    return pl.pallas_call(
        project_kernel,
        grid=(2, blocks),
        in_specs=[
            pl.BlockSpec((rows, size), lambda s, b: (0, b * (1 - s) + (blocks - 1) * s)),
            pl.BlockSpec((2, None, size, width), lambda s, b: (0, b * (1 - s) + (blocks - 1 - b) * s, 0, 0)),
            pl.BlockSpec((rows, 2 * width), lambda s, b: (0, 0)),
        ],
        out_specs=pl.BlockSpec((None, rows + NOTE, size), lambda s, b: ((blocks - 1 - b) * s + (blocks - 1) * (1 - s), 0, 0)),
        out_shape=jax.ShapeDtypeStruct((blocks, rows + NOTE, size), BF16),
        scratch_shapes=[
            pltpu.VMEM((rows, width), F32),
            pltpu.VMEM((rows, width), F32),
            pltpu.VMEM((8, width), F32),
        ],
        compiler_params=pltpu.CompilerParams(
            dimension_semantics=("arbitrary", "arbitrary"), vmem_limit_bytes=32 * 1024 * 1024
        ),
        cost_estimate=pl.CostEstimate(
            flops=8 * rows * total * width, bytes_accessed=8 * total * width, transcendentals=0
        ),
    )(hidden, projector, teacher)


def shards(teacher_in, teacher_weight, student_in, student_weight, projector):
    role = lax.axis_index("role")
    n_tensor = lax.axis_size("tensor")
    n_data = lax.axis_size("dp")
    own_rows = student_in.shape[0]
    total_rows = 2 * own_rows * n_data
    out_width = teacher_weight.shape[1]
    half = out_width // 2
    feat, hid = student_weight.shape
    wide = feat * n_data
    cols = projector.shape[1]
    model_from = sources("tensor")

    weight = lax.all_gather(student_weight, ("role", "dp"), axis=0, tiled=True)

    swap = [(d * 8 + t, t * 8 + d) for d in range(8) for t in range(8)]
    projector = lax.ppermute(projector, ("dp", "tensor"), swap)
    projector = lax.all_gather(projector, ("role", "dp"), axis=0, tiled=True)
    projector = projector.reshape(2, n_data, hid, cols)

    away = dot(lax.dynamic_index_in_dim(teacher_in, 1 - role, 0, False), teacher_weight)
    away = flip(away.astype(BF16))
    teacher = dot(lax.dynamic_index_in_dim(teacher_in, role, 0, False), teacher_weight)
    teacher = teacher + away.astype(F32)
    teacher = [
        jnp.concatenate(
            [lax.dynamic_slice_in_dim(teacher, h * half + s * cols, cols, axis=1) for h in (0, 1)],
            axis=1,
        )
        for s in model_from
    ]
    teacher = dict(zip(OFFSETS, teacher))
    t_got = [ring_pair(teacher, k, "tensor") for k in (1, -1, 2)]

    mine = lax.dynamic_slice_in_dim(student_in, role * wide, wide, axis=1)
    theirs = flip(lax.dynamic_slice_in_dim(student_in, (1 - role) * wide, wide, axis=1))

    weight, *t_near = lax.optimization_barrier((weight, teacher[0, 0], teacher[0, 1]))
    teacher[0, 0], teacher[0, 1] = t_near
    pre = dot(student_in, weight)
    sigma = jax.nn.sigmoid(pre)
    hidden = (pre * sigma).astype(BF16)
    hidden, *t_got[:2] = lax.optimization_barrier((hidden, *t_got[:2]))
    h_first = gather_start(hidden, "tensor")
    h_middle = gather_middle(hidden, h_first, "tensor")
    h_middle[0], t_got[2], theirs = lax.optimization_barrier((h_middle[0], t_got[2], theirs))
    hidden = place(gather_end(hidden, h_first, h_middle, "tensor"), model_from, 1)
    teacher = ring_end(teacher, t_got, "tensor")
    hidden, teacher = lax.optimization_barrier((hidden, teacher))
    student = jnp.concatenate([mine, theirs], axis=0)

    back = project(hidden, projector, teacher)
    back = lax.all_to_all(back, "tensor", 0, 0, tiled=True)
    back = jnp.sum(back.astype(F32), axis=0)
    square = join_note(back[own_rows:])
    back = back[:own_rows]

    delta = (back * sigma * (1.0 + pre * (1.0 - sigma))).astype(BF16)
    packed = flip(jnp.concatenate([delta, split_note(square, hid)], axis=0))
    delta = jnp.concatenate([delta, packed[:own_rows]], axis=0)
    square = square + join_note(packed[own_rows:])

    grad = dot(student, delta, ((0,), (0,))).astype(BF16).reshape(n_data, feat, hid)
    note = jnp.broadcast_to(split_note(square, hid)[None], (n_data, NOTE, hid))
    grad = jnp.concatenate([grad, note], axis=1)
    grad = lax.all_to_all(grad, "dp", 0, 0, tiled=True)
    grad = jnp.sum(grad.astype(F32), axis=0)
    loss = join_note(grad[feat:])[0, 0] / (2.0 * total_rows * out_width)
    return (grad[:feat] / jnp.sqrt(jnp.float32(total_rows)), loss)


def solution(mesh):
    in_specs = (
        P(None, "dp", ("role", "tensor")),
        P(("role", "tensor"), None),
        P(("role", "dp"), None),
        P(("role", "dp"), "tensor"),
        P("tensor", ("role", "dp")),
    )
    out_specs = (P(("role", "dp"), "tensor"), P())
    return jax.shard_map(shards, mesh=mesh, in_specs=in_specs, out_specs=out_specs, check_vma=False)
```

```python
import jax
import jax.numpy as jnp
from jax import lax
from jax.experimental import pallas as pl
from jax.experimental.pallas import tpu as pltpu
from jax.sharding import PartitionSpec as P

BF16 = jnp.bfloat16
F32 = jnp.float32
NOTE = 16
OFFSETS = ((0, 0), (0, 1), (1, 0), (-1, 0), (2, 0), (1, 1), (-1, 1), (2, 1))


def shift(value, axis, k, e):
    perm = [(i, ((i // 2 + k) % 4) * 2 + ((i % 2) ^ e)) for i in range(8)]
    return lax.ppermute(value, axis, perm)


def flip(value):
    return lax.ppermute(value, "role", [(0, 1), (1, 0)])


def sources(axis):
    me = lax.axis_index(axis)
    return [((((me >> 1) - k) & 3) << 1) | ((me & 1) ^ e) for k, e in OFFSETS]


def after(value, *others):
    return lax.optimization_barrier((value, *others))[0]


def gather_start(block, axis):
    return [shift(block, axis, 0, 1), shift(block, axis, 1, 0), shift(block, axis, -1, 0)]


def gather_middle(block, first, axis):
    other, before, nxt = first
    half = block.shape[0] // 2
    up = shift(jnp.concatenate([other, before[:half]], axis=0), axis, 1, 0)
    down = shift(jnp.concatenate([other, nxt[half:]], axis=0), axis, -1, 0)
    return [up, down]


def gather_end(block, first, middle, axis):
    other, before, nxt = first
    up, down = middle
    rows = block.shape[0]
    far = jnp.concatenate([up[rows:], down[rows:]], axis=0)
    other_far = shift(far, axis, 0, 1)
    return [block, other, before, nxt, far, up[:rows], down[:rows], other_far]


def ring_pair(by, k, axis):
    pair = jnp.concatenate([by[k, 0], by[k, 1]], axis=0).astype(BF16)
    return shift(pair, axis, -k, 0)


def ring_end(by, got, axis):
    rows = by[0, 0].shape[0]
    near, cross = by[0, 0].astype(F32), by[0, 1].astype(F32)
    for g in got:
        near = near + g[:rows].astype(F32)
        cross = cross + g[rows:].astype(F32)
    return near + shift(cross.astype(BF16), axis, 0, 1).astype(F32)


def dot(a, b, dims=((1,), (0,))):
    return lax.dot_general(a, b, (dims, ((), ())), preferred_element_type=F32)


def split_note(value, width):
    value = jnp.broadcast_to(value, (1, width)).astype(F32)
    row = lax.broadcasted_iota(jnp.int32, (NOTE, width), 0)
    high = lax.reduce_precision(value, 8, 7)
    middle = lax.reduce_precision(value - high, 8, 7)
    low = value - high - middle
    note = jnp.where(row == 0, high, jnp.where(row == 1, middle, jnp.where(row == 2, low, 0.0)))
    return note.astype(BF16)


def join_note(note):
    return jnp.sum(note.astype(F32), axis=0, keepdims=True)


def project_kernel(order, hidden, projector, teacher, out, low, high, square):
    step, block = pl.program_id(0), pl.program_id(1)
    n, width = out.shape[0] - NOTE, out.shape[1]

    @pl.when((step == 0) & (block == 0))
    def _():
        low[...] = jnp.zeros_like(low)
        high[...] = jnp.zeros_like(high)

    @pl.when(step == 0)
    def _():
        low[...] += jnp.dot(hidden[...], projector[0], preferred_element_type=F32)
        high[...] += jnp.dot(hidden[...], projector[1], preferred_element_type=F32)

    @pl.when((step == 1) & (block == 0))
    def _():
        low[...] -= teacher[:, :width]
        high[...] -= teacher[:, width:]
        square[...] = jnp.broadcast_to(
            jnp.sum(low[...] * low[...] + high[...] * high[...], keepdims=True), square.shape
        )

    @pl.when(step == 1)
    def _():
        dims = (((1,), (1,)), ((), ()))
        back = lax.dot_general(low[...].astype(BF16), projector[0], dims, preferred_element_type=F32)
        back += lax.dot_general(high[...].astype(BF16), projector[1], dims, preferred_element_type=F32)
        out[:n] = back.astype(BF16)
        value = square[:1]
        row = lax.broadcasted_iota(jnp.int32, (NOTE, width), 0)
        top = value.astype(BF16).astype(F32)
        middle = (value - top).astype(BF16).astype(F32)
        bottom = value - top - middle
        note = jnp.where(row == 0, top, jnp.where(row == 1, middle, jnp.where(row == 2, bottom, 0.0)))
        out[n:] = note.astype(BF16)


def project(order, hidden, projector, teacher):
    _, blocks, size, width = projector.shape
    rows = teacher.shape[0]
    last = blocks - 1
    return pl.pallas_call(
        project_kernel,
        grid_spec=pltpu.PrefetchScalarGridSpec(
            num_scalar_prefetch=1,
            grid=(2, blocks),
            in_specs=[
                pl.BlockSpec((rows, size), lambda s, b, order: (b * (1 - s) + last * s, 0)),
                pl.BlockSpec(
                    (2, None, size, width), lambda s, b, order: (0, b * (1 - s) + (last - b) * s, 0, 0)
                ),
                pl.BlockSpec((rows, 2 * width), lambda s, b, order: (0, 0)),
            ],
            out_specs=pl.BlockSpec((None, rows + NOTE, size), lambda s, b, order: (order[last - b * s], 0, 0)),
            scratch_shapes=[
                pltpu.VMEM((rows, width), F32),
                pltpu.VMEM((rows, width), F32),
                pltpu.VMEM((8, width), F32),
            ],
        ),
        out_shape=jax.ShapeDtypeStruct((blocks, rows + NOTE, size), BF16),
        compiler_params=pltpu.CompilerParams(
            dimension_semantics=("arbitrary", "arbitrary"), vmem_limit_bytes=32 * 1024 * 1024
        ),
        cost_estimate=pl.CostEstimate(
            flops=8 * rows * blocks * size * width, bytes_accessed=8 * blocks * size * width, transcendentals=0
        ),
    )(order, hidden, projector, teacher)


def teach_kernel(role, own, other, weight, out, away):
    out[...] = jnp.dot(own[...], weight[...], preferred_element_type=F32)
    away[...] = jnp.dot(other[...], weight[...], preferred_element_type=F32).astype(BF16)


def teach(role, teacher_in, weight, blocks, width):
    _, rows, depth = teacher_in.shape
    shape = (blocks, rows, 2 * width)
    place = pl.BlockSpec((None, rows, width), lambda j, role: (j % blocks, 0, j // blocks))
    return pl.pallas_call(
        teach_kernel,
        grid_spec=pltpu.PrefetchScalarGridSpec(
            num_scalar_prefetch=1,
            grid=(2 * blocks,),
            in_specs=[
                pl.BlockSpec((None, rows, depth), lambda j, role: (role[0], 0, 0)),
                pl.BlockSpec((None, rows, depth), lambda j, role: (1 - role[0], 0, 0)),
                pl.BlockSpec((depth, width), lambda j, role: (0, j)),
            ],
            out_specs=[place, place],
        ),
        out_shape=[jax.ShapeDtypeStruct(shape, F32), jax.ShapeDtypeStruct(shape, BF16)],
        compiler_params=pltpu.CompilerParams(
            dimension_semantics=("arbitrary",), vmem_limit_bytes=32 * 1024 * 1024
        ),
        cost_estimate=pl.CostEstimate(
            flops=8 * rows * depth * blocks * width, bytes_accessed=4 * depth * blocks * width, transcendentals=0
        ),
    )(role, teacher_in, teacher_in, weight)


def shards(teacher_in, teacher_weight, student_in, student_weight, projector):
    role = lax.axis_index("role")
    n_tensor = lax.axis_size("tensor")
    n_data = lax.axis_size("dp")
    own_rows = student_in.shape[0]
    total_rows = 2 * own_rows * n_data
    out_width = teacher_weight.shape[1]
    feat, hid = student_weight.shape
    wide = feat * n_data
    cols = projector.shape[1]
    model_from = sources("tensor")

    weight = lax.all_gather(student_weight, ("role", "dp"), axis=0, tiled=True)

    swap = []
    for d in range(8):
        for t in range(8):
            to = ((t // 2 - d // 2) % 4) * 2 + (t ^ d) % 2
            swap.append((d * 8 + t, to * 8 + d))
    projector = lax.ppermute(projector, ("dp", "tensor"), swap)

    own, away = teach(jnp.full((1,), role, jnp.int32), teacher_in, teacher_weight, n_tensor, cols)
    away = flip(away)
    teacher = [
        lax.dynamic_index_in_dim(own, s, 0, False) + lax.dynamic_index_in_dim(away, s, 0, False).astype(F32)
        for s in model_from
    ]
    teacher = dict(zip(OFFSETS, teacher))
    t_got = [ring_pair(teacher, k, "tensor") for k in (1, -1)]
    projector = lax.all_gather(after(projector, *t_got), ("role", "dp"), axis=0, tiled=True)
    projector = projector.reshape(2, n_data, hid, cols)
    weight, teacher[2, 0], *t_got = lax.optimization_barrier((weight, teacher[2, 0], *t_got))
    t_got.append(ring_pair(teacher, 2, "tensor"))

    pre = dot(student_in, weight)
    sigma = jax.nn.sigmoid(pre)
    hidden = (pre * sigma).astype(BF16)
    h_first = gather_start(hidden, "tensor")
    h_middle = gather_middle(hidden, h_first, "tensor")

    h_middle = list(lax.optimization_barrier((*h_middle, t_got[2])))
    t_got[2] = h_middle.pop()

    student = after(student_in, *h_middle)
    mine = lax.dynamic_slice_in_dim(student, role * wide, wide, axis=1)
    theirs = flip(lax.dynamic_slice_in_dim(student, (1 - role) * wide, wide, axis=1))

    hidden = dict(zip(OFFSETS, gather_end(hidden, h_first, h_middle, "tensor")))
    hidden = jnp.concatenate([hidden[k, e] for k in (0, -1, 2, 1) for e in (0, 1)], axis=0)
    teacher = ring_end(teacher, t_got, "tensor")
    hidden, teacher, mine, theirs = lax.optimization_barrier((hidden, teacher, mine, theirs))
    student = jnp.concatenate([mine, theirs], axis=0)

    me = lax.axis_index("tensor")
    order = [((((me >> 1) + b // 2) & 3) << 1) | ((me & 1) ^ (b % 2)) for b in range(n_tensor)]
    back = project(jnp.stack(order).astype(jnp.int32), hidden, projector, teacher)
    back = lax.all_to_all(back, "tensor", 0, 0, tiled=True)
    back = jnp.sum(back.astype(F32), axis=0)
    square = join_note(back[own_rows:])
    back = back[:own_rows]

    delta = (back * sigma * (1.0 + pre * (1.0 - sigma))).astype(BF16)
    packed = flip(jnp.concatenate([delta, split_note(square, hid)], axis=0))
    delta = jnp.concatenate([delta, packed[:own_rows]], axis=0)
    square = square + join_note(packed[own_rows:])

    grad = dot(student, delta, ((0,), (0,))).astype(BF16).reshape(n_data, feat, hid)
    note = jnp.broadcast_to(split_note(square, hid)[None], (n_data, NOTE, hid))
    grad = jnp.concatenate([grad, note], axis=1)
    grad = lax.all_to_all(grad, "dp", 0, 0, tiled=True)
    grad = jnp.sum(grad.astype(F32), axis=0)
    loss = join_note(grad[feat:])[0, 0] / (2.0 * total_rows * out_width)
    return (grad[:feat] / jnp.sqrt(jnp.float32(total_rows)), loss)


def solution(mesh):
    in_specs = (
        P(None, "dp", ("role", "tensor")),
        P(("role", "tensor"), None),
        P(("role", "dp"), None),
        P(("role", "dp"), "tensor"),
        P("tensor", ("role", "dp")),
    )
    out_specs = (P(("role", "dp"), "tensor"), P())
    return jax.shard_map(shards, mesh=mesh, in_specs=in_specs, out_specs=out_specs, check_vma=False)
```

```python
import jax
import jax.numpy as jnp
from jax import lax
from jax.experimental import pallas as pl
from jax.experimental.pallas import tpu as pltpu
from jax.sharding import PartitionSpec as P

BF16 = jnp.bfloat16
F32 = jnp.float32
NOTE = 16
OFFSETS = ((0, 0), (0, 1), (1, 0), (-1, 0), (2, 0), (1, 1), (-1, 1), (2, 1))


def shift(value, axis, k, e):
    perm = [(i, ((i // 2 + k) % 4) * 2 + ((i % 2) ^ e)) for i in range(8)]
    return lax.ppermute(value, axis, perm)


def flip(value):
    return lax.ppermute(value, "role", [(0, 1), (1, 0)])


def sources(axis):
    me = lax.axis_index(axis)
    return [((((me >> 1) - k) & 3) << 1) | ((me & 1) ^ e) for k, e in OFFSETS]


def after(value, *others):
    return lax.optimization_barrier((value, *others))[0]


def gather_start(block, axis):
    return [shift(block, axis, 0, 1), shift(block, axis, 1, 0), shift(block, axis, -1, 0)]


def gather_middle(block, first, axis):
    other, before, nxt = first
    half = block.shape[0] // 2
    up = shift(jnp.concatenate([other, before[:half]], axis=0), axis, 1, 0)
    down = shift(jnp.concatenate([other, nxt[half:]], axis=0), axis, -1, 0)
    return [up, down]


def gather_end(block, first, middle, axis):
    other, before, nxt = first
    up, down = middle
    rows = block.shape[0]
    far = jnp.concatenate([up[rows:], down[rows:]], axis=0)
    other_far = shift(far, axis, 0, 1)
    return [block, other, before, nxt, far, up[:rows], down[:rows], other_far]


def place(blocks, at, dim):
    size = blocks[0].shape[dim]
    shape = list(blocks[0].shape)
    shape[dim] = 8 * size
    out = jnp.zeros(shape, blocks[0].dtype)
    for block, s in zip(blocks, at):
        out = lax.dynamic_update_slice_in_dim(out, block, s * size, axis=dim)
    return out


def ring_pair(by, k, axis):
    pair = jnp.concatenate([by[k, 0], by[k, 1]], axis=0).astype(BF16)
    return shift(pair, axis, -k, 0)


def ring_end(by, got, axis):
    rows = by[0, 0].shape[0]
    near, cross = by[0, 0].astype(F32), by[0, 1].astype(F32)
    for g in got:
        near = near + g[:rows].astype(F32)
        cross = cross + g[rows:].astype(F32)
    return near + shift(cross.astype(BF16), axis, 0, 1).astype(F32)


def dot(a, b, dims=((1,), (0,))):
    return lax.dot_general(a, b, (dims, ((), ())), preferred_element_type=F32)


def split_note(value, width):
    value = jnp.broadcast_to(value, (1, width)).astype(F32)
    row = lax.broadcasted_iota(jnp.int32, (NOTE, width), 0)
    high = lax.reduce_precision(value, 8, 7)
    middle = lax.reduce_precision(value - high, 8, 7)
    low = value - high - middle
    note = jnp.where(row == 0, high, jnp.where(row == 1, middle, jnp.where(row == 2, low, 0.0)))
    return note.astype(BF16)


def join_note(note):
    return jnp.sum(note.astype(F32), axis=0, keepdims=True)


def project_kernel(order, hidden, whole, own, other, teacher, out, total, square):
    step, block = pl.program_id(0), pl.program_id(1)
    n, width = out.shape[0] - NOTE, out.shape[1]
    part = width // 2
    parts = (whole.at[0], whole.at[1], own, other)

    @pl.when((step == 0) & (block == 0))
    def _():
        first = order[order.shape[0] - 1] == 0
        late_low, late_high = teacher[:, part:width], teacher[:, width + part :]
        total[0] = -teacher[:, :part]
        total[1] = -teacher[:, width : width + part]
        total[2] = -jnp.where(first, late_low, late_high)
        total[3] = -jnp.where(first, late_high, late_low)

    @pl.when(step == 0)
    def _():
        for i, p in enumerate(parts):
            total[i] += jnp.dot(hidden[...], p[...], preferred_element_type=F32)

    @pl.when((step == 1) & (block == 0))
    def _():
        squares = jnp.sum(total[...] * total[...], axis=0)
        square[...] = jnp.broadcast_to(jnp.sum(squares, keepdims=True), square.shape)

    @pl.when(step == 1)
    def _():
        dims = (((1,), (1,)), ((), ()))
        back = sum(
            lax.dot_general(total[i].astype(BF16), p[...], dims, preferred_element_type=F32)
            for i, p in enumerate(parts)
        )
        out[:n] = back.astype(BF16)
        value = square[:1]
        row = lax.broadcasted_iota(jnp.int32, (NOTE, width), 0)
        top = value.astype(BF16).astype(F32)
        middle = (value - top).astype(BF16).astype(F32)
        bottom = value - top - middle
        note = jnp.where(row == 0, top, jnp.where(row == 1, middle, jnp.where(row == 2, bottom, 0.0)))
        out[n:] = note.astype(BF16)


def project(order, hidden, whole, own, other, teacher):
    blocks, size, part = own.shape
    rows = teacher.shape[0]
    last = blocks - 1

    def at(s, b):
        return b * (1 - s) + (last - b) * s

    return pl.pallas_call(
        project_kernel,
        grid_spec=pltpu.PrefetchScalarGridSpec(
            num_scalar_prefetch=1,
            grid=(2, blocks),
            in_specs=[
                pl.BlockSpec((rows, size), lambda s, b, order: (b * (1 - s) + last * s, 0)),
                pl.BlockSpec((2, None, size, part), lambda s, b, order: (0, at(s, b), 0, 0)),
                pl.BlockSpec((None, size, part), lambda s, b, order: (at(s, b), 0, 0)),
                pl.BlockSpec((None, size, part), lambda s, b, order: (at(s, b), 0, 0)),
                pl.BlockSpec((rows, 4 * part), lambda s, b, order: (0, 0)),
            ],
            out_specs=pl.BlockSpec((None, rows + NOTE, size), lambda s, b, order: (order[last - b * s], 0, 0)),
            scratch_shapes=[pltpu.VMEM((4, rows, part), F32), pltpu.VMEM((8, size), F32)],
        ),
        out_shape=jax.ShapeDtypeStruct((blocks, rows + NOTE, size), BF16),
        compiler_params=pltpu.CompilerParams(
            dimension_semantics=("arbitrary", "arbitrary"), vmem_limit_bytes=32 * 1024 * 1024
        ),
        cost_estimate=pl.CostEstimate(
            flops=16 * rows * blocks * size * part, bytes_accessed=16 * blocks * size * part, transcendentals=0
        ),
    )(order, hidden, whole, own, other, teacher)


def teach_kernel(role, tokens, weight, out, away):
    product = jnp.dot(tokens[...], weight[...], preferred_element_type=F32)
    rows = out.shape[0]
    first = role[0] == 0
    out[...] = jnp.where(first, product[:rows], product[rows:])
    away[...] = jnp.where(first, product[rows:], product[:rows]).astype(BF16)


def teach(role, teacher_in, weight, blocks, width):
    _, rows, depth = teacher_in.shape
    shape = (blocks, rows, 2 * width)
    place = pl.BlockSpec((None, rows, width), lambda j, role: (j % blocks, 0, j // blocks))
    return pl.pallas_call(
        teach_kernel,
        grid_spec=pltpu.PrefetchScalarGridSpec(
            num_scalar_prefetch=1,
            grid=(2 * blocks,),
            in_specs=[
                pl.BlockSpec((2 * rows, depth), lambda j, role: (0, 0)),
                pl.BlockSpec((depth, width), lambda j, role: (0, j)),
            ],
            out_specs=[place, place],
        ),
        out_shape=[jax.ShapeDtypeStruct(shape, F32), jax.ShapeDtypeStruct(shape, BF16)],
        compiler_params=pltpu.CompilerParams(
            dimension_semantics=("arbitrary",), vmem_limit_bytes=32 * 1024 * 1024
        ),
        cost_estimate=pl.CostEstimate(
            flops=8 * rows * depth * blocks * width, bytes_accessed=4 * depth * blocks * width, transcendentals=0
        ),
    )(role, teacher_in.reshape(2 * rows, depth), weight)


def shards(teacher_in, teacher_weight, student_in, student_weight, projector):
    role = lax.axis_index("role")
    n_tensor = lax.axis_size("tensor")
    n_data = lax.axis_size("dp")
    own_rows = student_in.shape[0]
    total_rows = 2 * own_rows * n_data
    out_width = teacher_weight.shape[1]
    feat, hid = student_weight.shape
    wide = feat * n_data
    cols = projector.shape[1]
    model_from = sources("tensor")

    weight = lax.all_gather(student_weight, ("role", "dp"), axis=0, tiled=True)

    swap = []
    for d in range(8):
        for t in range(8):
            to = ((t // 2 - d // 2) % 4) * 2 + (t ^ d) % 2
            swap.append((d * 8 + t, to * 8 + d))
    projector = lax.ppermute(projector, ("dp", "tensor"), swap)

    own, away = teach(jnp.full((1,), role, jnp.int32), teacher_in, teacher_weight, n_tensor, cols)
    away, projector = lax.optimization_barrier((flip(away), projector))
    teacher = [
        lax.dynamic_index_in_dim(own, s, 0, False) + lax.dynamic_index_in_dim(away, s, 0, False).astype(F32)
        for s in model_from
    ]
    teacher = dict(zip(OFFSETS, teacher))
    t_got = [ring_pair(teacher, k, "tensor") for k in (1, -1)]

    part = cols // 2
    p_ring, p_whole = lax.optimization_barrier((projector[:, part:], projector[:, :part]))
    p_first = gather_start(p_ring, "dp")
    p_whole = lax.all_gather(p_whole, ("role", "dp"), axis=0, tiled=True)
    p_whole = p_whole.reshape(2, n_data, hid, part)

    mine = lax.dynamic_slice_in_dim(student_in, role * wide, wide, axis=1)
    theirs = lax.dynamic_slice_in_dim(student_in, (1 - role) * wide, wide, axis=1)
    mine, theirs, *p_first = lax.optimization_barrier((mine, theirs, *p_first))
    theirs = flip(theirs)

    weight, teacher[2, 0], *t_got = lax.optimization_barrier((weight, teacher[2, 0], *t_got))
    p_middle = gather_middle(p_ring, p_first, "dp")
    pre = dot(student_in, weight)
    sigma = jax.nn.sigmoid(pre)
    hidden = (pre * sigma).astype(BF16)
    hidden, *p_middle = lax.optimization_barrier((hidden, *p_middle))
    h_first = gather_start(hidden, "tensor")
    t_got.append(ring_pair(teacher, 2, "tensor"))
    h_middle = gather_middle(hidden, h_first, "tensor")
    p_own = place(gather_end(p_ring, p_first, p_middle, "dp"), sources("dp"), 0)
    p_other = flip(p_own)

    hidden = dict(zip(OFFSETS, gather_end(hidden, h_first, h_middle, "tensor")))
    hidden = jnp.concatenate([hidden[k, e] for k in (0, -1, 2, 1) for e in (0, 1)], axis=0)
    teacher = ring_end(teacher, t_got, "tensor")
    hidden, teacher, p_own, p_other, theirs = lax.optimization_barrier((hidden, teacher, p_own, p_other, theirs))
    student = jnp.concatenate([mine, theirs], axis=0)

    me = lax.axis_index("tensor")
    order = [((((me >> 1) + b // 2) & 3) << 1) | ((me & 1) ^ (b % 2)) for b in range(n_tensor)]
    order = jnp.stack(order + [role]).astype(jnp.int32)
    p_own, p_other = p_own.reshape(n_data, hid, part), p_other.reshape(n_data, hid, part)
    back = project(order, hidden, p_whole, p_own, p_other, teacher)
    back = lax.all_to_all(back, "tensor", 0, 0, tiled=True)
    back = jnp.sum(back.astype(F32), axis=0)
    square = join_note(back[own_rows:])
    back = back[:own_rows]

    delta = (back * sigma * (1.0 + pre * (1.0 - sigma))).astype(BF16)
    packed = flip(jnp.concatenate([delta, split_note(square, hid)], axis=0))
    delta = jnp.concatenate([delta, packed[:own_rows]], axis=0)
    square = square + join_note(packed[own_rows:])

    grad = dot(student, delta, ((0,), (0,))).astype(BF16).reshape(n_data, feat, hid)
    note = jnp.broadcast_to(split_note(square, hid)[None], (n_data, NOTE, hid))
    grad = jnp.concatenate([grad, note], axis=1)
    grad = lax.all_to_all(grad, "dp", 0, 0, tiled=True)
    grad = jnp.sum(grad.astype(F32), axis=0)
    loss = join_note(grad[feat:])[0, 0] / (2.0 * total_rows * out_width)
    return (grad[:feat] / jnp.sqrt(jnp.float32(total_rows)), loss)


def solution(mesh):
    in_specs = (
        P(None, "dp", ("role", "tensor")),
        P(("role", "tensor"), None),
        P(("role", "dp"), None),
        P(("role", "dp"), "tensor"),
        P("tensor", ("role", "dp")),
    )
    out_specs = (P(("role", "dp"), "tensor"), P())
    return jax.shard_map(shards, mesh=mesh, in_specs=in_specs, out_specs=out_specs, check_vma=False)
```

```python
import jax
import jax.numpy as jnp
from jax import lax
from jax.experimental import pallas as pl
from jax.experimental.pallas import tpu as pltpu
from jax.sharding import PartitionSpec as P

BF16 = jnp.bfloat16
F32 = jnp.float32
NOTE = 16
OFFSETS = ((0, 0), (0, 1), (1, 0), (-1, 0), (2, 0), (1, 1), (-1, 1), (2, 1))


def shift(value, axis, k, e):
    perm = [(i, ((i // 2 + k) % 4) * 2 + ((i % 2) ^ e)) for i in range(8)]
    return lax.ppermute(value, axis, perm)


def flip(value):
    return lax.ppermute(value, "role", [(0, 1), (1, 0)])


def sources(axis):
    me = lax.axis_index(axis)
    return [((((me >> 1) - k) & 3) << 1) | ((me & 1) ^ e) for k, e in OFFSETS]


def after(value, *others):
    return lax.optimization_barrier((value, *others))[0]


def gather_start(block, axis):
    return [shift(block, axis, 0, 1), shift(block, axis, 1, 0), shift(block, axis, -1, 0)]


def gather_middle(block, first, axis):
    other, before, nxt = first
    half = block.shape[0] // 2
    up = shift(jnp.concatenate([other, before[:half]], axis=0), axis, 1, 0)
    down = shift(jnp.concatenate([other, nxt[half:]], axis=0), axis, -1, 0)
    return [up, down]


def gather_end(block, first, middle, axis):
    other, before, nxt = first
    up, down = middle
    rows = block.shape[0]
    far = jnp.concatenate([up[rows:], down[rows:]], axis=0)
    other_far = shift(far, axis, 0, 1)
    return [block, other, before, nxt, far, up[:rows], down[:rows], other_far]


def place(blocks, at, dim):
    size = blocks[0].shape[dim]
    shape = list(blocks[0].shape)
    shape[dim] = 8 * size
    out = jnp.zeros(shape, blocks[0].dtype)
    for block, s in zip(blocks, at):
        out = lax.dynamic_update_slice_in_dim(out, block, s * size, axis=dim)
    return out


def dot(a, b, dims=((1,), (0,))):
    return lax.dot_general(a, b, (dims, ((), ())), preferred_element_type=F32)


def split_note(value, width):
    value = jnp.broadcast_to(value, (1, width)).astype(F32)
    row = lax.broadcasted_iota(jnp.int32, (NOTE, width), 0)
    high = lax.reduce_precision(value, 8, 7)
    middle = lax.reduce_precision(value - high, 8, 7)
    low = value - high - middle
    note = jnp.where(row == 0, high, jnp.where(row == 1, middle, jnp.where(row == 2, low, 0.0)))
    return note.astype(BF16)


def join_note(note):
    return jnp.sum(note.astype(F32), axis=0, keepdims=True)


def project_kernel(order, hidden, own, other, teacher, out, total, kept, square):
    step, block = pl.program_id(0), pl.program_id(1)
    n, width = out.shape[0] - NOTE, out.shape[1]
    size = own.shape[0]

    @pl.when((step == 0) & (block == 0))
    def _():
        first = order[order.shape[0] - 1] == 0
        low, high = teacher[:, :width], teacher[:, width:]
        total[0] = -jnp.where(first, low, high)
        total[1] = -jnp.where(first, high, low)

    @pl.when(step == 0)
    def _():
        kept[0, block] = own[...]
        kept[1, block] = other[...]
        total[0] += jnp.dot(hidden[...], own[...], preferred_element_type=F32)
        total[1] += jnp.dot(hidden[...], other[...], preferred_element_type=F32)

    @pl.when((step == 1) & (block == 0))
    def _():
        squares = total[0] * total[0] + total[1] * total[1]
        square[...] = jnp.broadcast_to(jnp.sum(squares, keepdims=True), square.shape)

    @pl.when(step == 1)
    def _():
        dims = (((1,), (1,)), ((), ()))
        back = lax.dot_general(total[0].astype(BF16), kept[0, block], dims, preferred_element_type=F32)
        back += lax.dot_general(total[1].astype(BF16), kept[1, block], dims, preferred_element_type=F32)
        out[:n] = back.astype(BF16)
        value = square[:1]
        row = lax.broadcasted_iota(jnp.int32, (NOTE, width), 0)
        top = value.astype(BF16).astype(F32)
        middle = (value - top).astype(BF16).astype(F32)
        bottom = value - top - middle
        note = jnp.where(row == 0, top, jnp.where(row == 1, middle, jnp.where(row == 2, bottom, 0.0)))
        out[n:] = note.astype(BF16)


def project(order, hidden, own, other, teacher):
    blocks, size, width = own.shape
    rows = teacher.shape[0]
    last = blocks - 1
    p_spec = pl.BlockSpec(
        (None, size, width), lambda s, b, order: (order[blocks + b * (1 - s) + last * s], 0, 0)
    )
    return pl.pallas_call(
        project_kernel,
        grid_spec=pltpu.PrefetchScalarGridSpec(
            num_scalar_prefetch=1,
            grid=(2, blocks),
            in_specs=[
                pl.BlockSpec((None, rows, size), lambda s, b, order: (order[b * (1 - s) + last * s], 0, 0)),
                p_spec,
                p_spec,
                pl.BlockSpec((rows, 2 * width), lambda s, b, order: (0, 0)),
            ],
            out_specs=pl.BlockSpec((None, rows + NOTE, size), lambda s, b, order: (order[2 * blocks + b * s], 0, 0)),
            scratch_shapes=[
                pltpu.VMEM((2, rows, width), F32),
                pltpu.VMEM((2, blocks, size, width), BF16),
                pltpu.VMEM((8, size), F32),
            ],
        ),
        out_shape=jax.ShapeDtypeStruct((blocks, rows + NOTE, size), BF16),
        compiler_params=pltpu.CompilerParams(
            dimension_semantics=("arbitrary", "arbitrary"), vmem_limit_bytes=32 * 1024 * 1024
        ),
        cost_estimate=pl.CostEstimate(
            flops=8 * rows * blocks * size * width, bytes_accessed=4 * blocks * size * width, transcendentals=0
        ),
    )(order, hidden, own, other, teacher)


def teach_kernel(role, tokens, weight, out, away):
    product = jnp.dot(tokens[...], weight[...], preferred_element_type=F32)
    count, rows, width = out.shape
    first = role[0] == 0
    for i in range(count):
        low, high = product[:rows, i * width : (i + 1) * width], product[rows:, i * width : (i + 1) * width]
        out[i] = jnp.where(first, low, high)
        away[i] = jnp.where(first, high, low).astype(BF16)


def teach(role, teacher_in, weight, blocks, width):
    _, rows, depth = teacher_in.shape
    shape = (blocks, rows, 2 * width)
    count = 4
    steps = blocks // count
    place = pl.BlockSpec((count, rows, width), lambda j, role: (j % steps, 0, j // steps))
    return pl.pallas_call(
        teach_kernel,
        grid_spec=pltpu.PrefetchScalarGridSpec(
            num_scalar_prefetch=1,
            grid=(2 * steps,),
            in_specs=[
                pl.BlockSpec((2 * rows, depth), lambda j, role: (0, 0)),
                pl.BlockSpec((depth, count * width), lambda j, role: (0, j)),
            ],
            out_specs=[place, place],
        ),
        out_shape=[jax.ShapeDtypeStruct(shape, F32), jax.ShapeDtypeStruct(shape, BF16)],
        compiler_params=pltpu.CompilerParams(
            dimension_semantics=("arbitrary",), vmem_limit_bytes=40 * 1024 * 1024
        ),
        cost_estimate=pl.CostEstimate(
            flops=8 * rows * depth * blocks * width, bytes_accessed=4 * depth * blocks * width, transcendentals=0
        ),
    )(role, teacher_in.reshape(2 * rows, depth), weight)


def shards(teacher_in, teacher_weight, student_in, student_weight, projector):
    role = lax.axis_index("role")
    n_tensor = lax.axis_size("tensor")
    n_data = lax.axis_size("dp")
    own_rows = student_in.shape[0]
    total_rows = 2 * own_rows * n_data
    out_width = teacher_weight.shape[1]
    feat, hid = student_weight.shape
    wide = feat * n_data
    cols = projector.shape[1]

    xh = lax.axis_index("tensor") & 1

    w_first = gather_start(student_weight, "dp")

    swap = []
    for d in range(8):
        for t in range(8):
            to = ((t // 2 - d // 2) % 4) * 2 + (t ^ d) % 2
            swap.append((d * 8 + t, to * 8 + d))
    projector = lax.ppermute(projector, ("dp", "tensor"), swap)

    own, away = teach(jnp.full((1,), role, jnp.int32), teacher_in, teacher_weight, n_tensor, cols)
    away, projector, *w_first = lax.optimization_barrier((away, projector, *w_first))
    away = flip(away)

    w_middle = gather_middle(student_weight, w_first, "dp")
    p_other = shift(projector, "dp", 0, 1)

    mine = lax.dynamic_slice_in_dim(student_in, role * wide, wide, axis=1)
    theirs = flip(lax.dynamic_slice_in_dim(student_in, (1 - role) * wide, wide, axis=1))

    zt = lax.axis_index("tensor") >> 1
    teacher = {}
    for k in (0, 1, -1, 2):
        at = ((zt - k) & 3) * 2
        pair = lax.dynamic_slice_in_dim(own, at, 2, axis=0) + lax.dynamic_slice_in_dim(away, at, 2, axis=0).astype(F32)
        teacher[k] = pair if k == 0 else pair.astype(BF16)
    teacher[1], teacher[-1], theirs, p_other, *w_middle = lax.optimization_barrier(
        (teacher[1], teacher[-1], theirs, p_other, *w_middle)
    )
    for k in (1, -1):
        teacher[k] = shift(teacher[k], "tensor", -k, 0)

    weight = gather_end(student_weight, w_first, w_middle, "dp")
    p_first = [shift(projector, "dp", 1, 0), shift(projector, "dp", -1, 0)]
    weight[-1], *p_first = lax.optimization_barrier((weight[-1], *p_first))
    p_first = [p_other, *p_first]

    weight = place(weight, sources("dp"), 0)
    student = jnp.concatenate([mine, theirs], axis=0)
    pre = dot(student, weight)
    pre = pre[:own_rows] + flip(pre[own_rows:])
    sigma = jax.nn.sigmoid(pre)
    hidden = (pre * sigma).astype(BF16)

    p_middle = gather_middle(projector, p_first, "dp")
    hidden, teacher[1], teacher[-1], teacher[2] = lax.optimization_barrier(
        (hidden, teacher[1], teacher[-1], teacher[2])
    )
    h_other = shift(hidden, "tensor", 0, 1)
    teacher[2] = shift(teacher[2], "tensor", 2, 0)
    h_other, *p_middle = lax.optimization_barrier((h_other, *p_middle))
    h_pair = jnp.concatenate([hidden, h_other], axis=0)
    h_before, h_after = shift(h_pair, "tensor", 1, 0), shift(h_pair, "tensor", -1, 0)
    p_own = gather_end(projector, p_first, p_middle, "dp")
    h_before, h_after, teacher[2], p_own[-1] = lax.optimization_barrier((h_before, h_after, teacher[2], p_own[-1]))
    h_far = jnp.concatenate(
        [shift(h_before[:own_rows], "tensor", 1, 0), shift(h_after[own_rows:], "tensor", -1, 0)], axis=0
    )
    p_own = place(p_own, sources("dp"), 0)
    p_flip = flip(p_own)
    hidden = jnp.concatenate([h_pair, h_after, h_far, h_before], axis=0).reshape(n_tensor, own_rows, hid)
    p_own, p_flip = p_own.reshape(n_data, hid, cols), p_flip.reshape(n_data, hid, cols)

    teacher = teacher[0] + sum(teacher[k].astype(F32) for k in (1, -1, 2))
    cross = lax.dynamic_index_in_dim(teacher, 1 - xh, 0, False).astype(BF16)
    teacher = lax.dynamic_index_in_dim(teacher, xh, 0, False) + shift(cross, "tensor", 0, 1).astype(F32)

    order = (
        list(range(n_tensor))
        + list(range(n_data))
        + [(((zt + b // 2) & 3) * 2) + ((b % 2) ^ xh) for b in range(n_tensor)]
        + [role]
    )
    order = jnp.stack([jnp.asarray(x, jnp.int32) for x in order])
    back = project(order, hidden, p_own, p_flip, teacher)
    back = lax.all_to_all(back, "tensor", 0, 0, tiled=True)
    back = jnp.sum(back.astype(F32), axis=0)
    square = join_note(back[own_rows:])
    back = back[:own_rows]

    delta = (back * sigma * (1.0 + pre * (1.0 - sigma))).astype(BF16)
    packed = flip(jnp.concatenate([delta, split_note(square, hid)], axis=0))
    delta = jnp.concatenate([delta, packed[:own_rows]], axis=0)
    square = square + join_note(packed[own_rows:])

    grad = dot(student, delta, ((0,), (0,))).astype(BF16).reshape(n_data, feat, hid)
    note = jnp.broadcast_to(split_note(square, hid)[None], (n_data, NOTE, hid))
    grad = jnp.concatenate([grad, note], axis=1)
    grad = lax.all_to_all(grad, "dp", 0, 0, tiled=True)
    grad = jnp.sum(grad.astype(F32), axis=0)
    loss = join_note(grad[feat:])[0, 0] / (2.0 * total_rows * out_width)
    return (grad[:feat] / jnp.sqrt(jnp.float32(total_rows)), loss)


def solution(mesh):
    in_specs = (
        P(None, "dp", ("role", "tensor")),
        P(("role", "tensor"), None),
        P(("role", "dp"), None),
        P(("role", "dp"), "tensor"),
        P("tensor", ("role", "dp")),
    )
    out_specs = (P(("role", "dp"), "tensor"), P())
    return jax.shard_map(shards, mesh=mesh, in_specs=in_specs, out_specs=out_specs, check_vma=False)
```

```python
import jax
import jax.numpy as jnp
from jax import lax
from jax.experimental import pallas as pl
from jax.experimental.pallas import tpu as pltpu
from jax.sharding import PartitionSpec as P

BF16 = jnp.bfloat16
F32 = jnp.float32
NOTE = 16
OFFSETS = ((0, 0), (0, 1), (1, 0), (-1, 0), (2, 0), (1, 1), (-1, 1), (2, 1))


def shift(value, axis, k, e):
    perm = [(i, ((i // 2 + k) % 4) * 2 + ((i % 2) ^ e)) for i in range(8)]
    return lax.ppermute(value, axis, perm)


def flip(value):
    return lax.ppermute(value, "role", [(0, 1), (1, 0)])


def sources(axis):
    me = lax.axis_index(axis)
    return [((((me >> 1) - k) & 3) << 1) | ((me & 1) ^ e) for k, e in OFFSETS]


def after(value, *others):
    return lax.optimization_barrier((value, *others))[0]


def gather_start(block, axis):
    return [shift(block, axis, 0, 1), shift(block, axis, 1, 0), shift(block, axis, -1, 0)]


def gather_middle(block, first, axis):
    other, before, nxt = first
    half = block.shape[0] // 2
    up = shift(jnp.concatenate([other, before[:half]], axis=0), axis, 1, 0)
    down = shift(jnp.concatenate([other, nxt[half:]], axis=0), axis, -1, 0)
    return [up, down]


def dot(a, b, dims=((1,), (0,))):
    return lax.dot_general(a, b, (dims, ((), ())), preferred_element_type=F32)


def split_note(value, width):
    value = jnp.broadcast_to(value, (1, width)).astype(F32)
    row = lax.broadcasted_iota(jnp.int32, (NOTE, width), 0)
    high = lax.reduce_precision(value, 8, 7)
    middle = lax.reduce_precision(value - high, 8, 7)
    low = value - high - middle
    note = jnp.where(row == 0, high, jnp.where(row == 1, middle, jnp.where(row == 2, low, 0.0)))
    return note.astype(BF16)


def join_note(note):
    return jnp.sum(note.astype(F32), axis=0, keepdims=True)


def project_kernel(order, *refs):
    h_refs, own_refs, other_refs = refs[:6], refs[6:13], refs[13:15]
    teacher, out, h_kept, p_kept, total, residual, h_sem, p_sem = refs[15:]
    n, width = out.shape[1] - NOTE, out.shape[2]
    size = p_kept.shape[2]
    half = size // 2
    lengths = [size] * 4 + [size + half] * 2 + [size]
    starts = [0, size, 2 * size, 3 * size, 0, size + half, 2 * (size + half)]
    other_refs = [
        other_refs[i // 4].at[pl.ds(at, length)] for i, (at, length) in enumerate(zip(starts, lengths))
    ]
    h_copies = []
    for i, (ref, at, count) in enumerate(zip(h_refs, (0, 1, 2, 4, 5, 6), (1, 1, 2, 1, 1, 2))):
        h_copies.append(pltpu.make_async_copy(ref, h_kept.at[pl.ds(at, count)], h_sem.at[i]))
    for copy in h_copies:
        copy.start()

    low, high = pl.ds(0, half), pl.ds(half, half)

    def pieces(parts):
        block, other, before, nxt, up, down, far = parts
        for whole in (block, other, before, nxt):
            yield whole.at[low], whole.at[high]
        yield up.at[pl.ds(size, half)], down.at[pl.ds(size, half)]
        for whole in (up, down, far):
            yield whole.at[low], whole.at[high]

    for j, sources_ in enumerate(zip(pieces(own_refs), pieces(other_refs))):
        for side, halves in enumerate(sources_):
            for part, source in enumerate(halves):
                target = p_kept.at[side, j, pl.ds(part * half, half)]
                pltpu.make_async_copy(source, target, p_sem.at[side, j, part]).start()

    first = order[16] == 0
    t_low, t_high = teacher[:, :width], teacher[:, width:]
    total[0] = -jnp.where(first, t_low, t_high)
    total[1] = -jnp.where(first, t_high, t_low)
    for copy in h_copies:
        copy.wait()

    @pl.loop(0, 8)
    def _(j):
        h = h_kept[order[j]]
        for side in range(2):
            for part in range(2):
                target = p_kept.at[side, j, pl.ds(part * half, half)]
                pltpu.make_async_copy(target, target, p_sem.at[side, j, part]).wait()
            total[side] += jnp.dot(h, p_kept[side, j], preferred_element_type=F32)

    squares = total[0] * total[0] + total[1] * total[1]
    value = jnp.broadcast_to(jnp.sum(squares, keepdims=True), (1, width))
    residual[...] = total[...].astype(BF16)
    row = lax.broadcasted_iota(jnp.int32, (NOTE, width), 0)
    top = value.astype(BF16).astype(F32)
    middle = (value - top).astype(BF16).astype(F32)
    bottom = value - top - middle
    note = jnp.where(row == 0, top, jnp.where(row == 1, middle, jnp.where(row == 2, bottom, 0.0)))
    note = note.astype(BF16)

    @pl.loop(0, 8)
    def _(j):
        dims = (((1,), (1,)), ((), ()))
        back = lax.dot_general(residual[0], p_kept[0, j], dims, preferred_element_type=F32)
        back += lax.dot_general(residual[1], p_kept[1, j], dims, preferred_element_type=F32)
        out[order[8 + j], :n] = back.astype(BF16)
        out[order[8 + j], n:] = note


def project(order, hidden, own, other, teacher):
    size, width = own[0].shape
    rows = teacher.shape[0]
    anywhere = pl.BlockSpec(memory_space=pl.ANY)
    inside = pl.BlockSpec(memory_space=pltpu.VMEM)
    return pl.pallas_call(
        project_kernel,
        in_specs=[pl.BlockSpec(memory_space=pltpu.SMEM)] + [anywhere] * 15 + [inside],
        out_specs=inside,
        scratch_shapes=[
            pltpu.VMEM((8, rows, size), BF16),
            pltpu.VMEM((2, 8, size, width), BF16),
            pltpu.VMEM((2, rows, width), F32),
            pltpu.VMEM((2, rows, width), BF16),
            pltpu.SemaphoreType.DMA((6,)),
            pltpu.SemaphoreType.DMA((2, 8, 2)),
        ],
        out_shape=jax.ShapeDtypeStruct((8, rows + NOTE, size), BF16),
        compiler_params=pltpu.CompilerParams(vmem_limit_bytes=32 * 1024 * 1024),
        cost_estimate=pl.CostEstimate(
            flops=64 * rows * size * width, bytes_accessed=32 * size * width, transcendentals=0
        ),
    )(order, *hidden, *own, *other, teacher)


def teach_kernel(role, tokens, weight, out, away):
    product = jnp.dot(tokens[...], weight[...], preferred_element_type=F32)
    count, rows, width = out.shape
    first = role[0] == 0
    for i in range(count):
        low, high = product[:rows, i * width : (i + 1) * width], product[rows:, i * width : (i + 1) * width]
        out[i] = jnp.where(first, low, high)
        away[i] = jnp.where(first, high, low).astype(BF16)


def teach(role, teacher_in, weight, blocks, width):
    _, rows, depth = teacher_in.shape
    shape = (blocks, rows, 2 * width)
    count = 4
    steps = blocks // count
    place = pl.BlockSpec((count, rows, width), lambda j, role: (j % steps, 0, j // steps))
    return pl.pallas_call(
        teach_kernel,
        grid_spec=pltpu.PrefetchScalarGridSpec(
            num_scalar_prefetch=1,
            grid=(2 * steps,),
            in_specs=[
                pl.BlockSpec((2 * rows, depth), lambda j, role: (0, 0)),
                pl.BlockSpec((depth, count * width), lambda j, role: (0, j)),
            ],
            out_specs=[place, place],
        ),
        out_shape=[jax.ShapeDtypeStruct(shape, F32), jax.ShapeDtypeStruct(shape, BF16)],
        compiler_params=pltpu.CompilerParams(
            dimension_semantics=("arbitrary",), vmem_limit_bytes=40 * 1024 * 1024
        ),
        cost_estimate=pl.CostEstimate(
            flops=8 * rows * depth * blocks * width, bytes_accessed=4 * depth * blocks * width, transcendentals=0
        ),
    )(role, teacher_in.reshape(2 * rows, depth), weight)


def shards(teacher_in, teacher_weight, student_in, student_weight, projector):
    role = lax.axis_index("role")
    n_tensor = lax.axis_size("tensor")
    n_data = lax.axis_size("dp")
    own_rows = student_in.shape[0]
    total_rows = 2 * own_rows * n_data
    out_width = teacher_weight.shape[1]
    feat, hid = student_weight.shape
    wide = feat * n_data
    cols = projector.shape[1]

    xh = lax.axis_index("tensor") & 1

    w_first = gather_start(student_weight, "dp")

    swap = []
    for d in range(8):
        for t in range(8):
            to = ((t // 2 - d // 2) % 4) * 2 + (t ^ d) % 2
            swap.append((d * 8 + t, to * 8 + d))
    projector = lax.ppermute(projector, ("dp", "tensor"), swap)

    own, away = teach(jnp.full((1,), role, jnp.int32), teacher_in, teacher_weight, n_tensor, cols)
    away, projector, *w_first = lax.optimization_barrier((away, projector, *w_first))
    away = flip(away)

    w_middle = gather_middle(student_weight, w_first, "dp")
    p_other = shift(projector, "dp", 0, 1)

    mine = lax.dynamic_slice_in_dim(student_in, role * wide, wide, axis=1)
    theirs = flip(lax.dynamic_slice_in_dim(student_in, (1 - role) * wide, wide, axis=1))

    zt = lax.axis_index("tensor") >> 1
    teacher = {}
    for k in (0, 1, -1, 2):
        at = ((zt - k) & 3) * 2
        pair = lax.dynamic_slice_in_dim(own, at, 2, axis=0) + lax.dynamic_slice_in_dim(away, at, 2, axis=0).astype(F32)
        teacher[k] = pair if k == 0 else pair.astype(BF16)
    teacher[0], teacher[1], teacher[-1], teacher[2] = lax.optimization_barrier(
        (teacher[0], teacher[1], teacher[-1], teacher[2])
    )

    projector, p_other, theirs, teacher[1], teacher[-1], *w_middle = lax.optimization_barrier(
        (projector, p_other, theirs, teacher[1], teacher[-1], *w_middle)
    )
    for k in (1, -1):
        teacher[k] = shift(teacher[k], "tensor", -k, 0)
    student = jnp.concatenate([mine, theirs], axis=0)
    up, down = w_middle
    w_far = shift(jnp.concatenate([up[feat:], down[feat:]], axis=0), "dp", 0, 1)
    p_first = [shift(projector, "dp", 1, 0), shift(projector, "dp", -1, 0)]
    w_far, *p_first = lax.optimization_barrier((w_far, *p_first))
    p_first = [p_other, *p_first]

    part = feat // 2
    at = sources("dp")
    pre = 0.0
    for j, block in enumerate((student_weight, *w_first, None, up[:feat], down[:feat], w_far)):
        columns = lax.dynamic_slice_in_dim(student, at[j] * feat, feat, axis=1)
        if block is None:
            pre = pre + dot(columns[:, :part], up[feat:]) + dot(columns[:, part:], down[feat:])
        else:
            pre = pre + dot(columns, block)
    pre = pre[:own_rows] + flip(pre[own_rows:])
    sigma = jax.nn.sigmoid(pre)
    hidden = (pre * sigma).astype(BF16)

    p_middle = gather_middle(projector, p_first, "dp")
    hidden, teacher[1], teacher[-1], teacher[2] = lax.optimization_barrier(
        (hidden, teacher[1], teacher[-1], teacher[2])
    )
    h_other = shift(hidden, "tensor", 0, 1)
    teacher[2] = shift(teacher[2], "tensor", 2, 0)
    near = lax.optimization_barrier(teacher[0] + teacher[1].astype(F32) + teacher[-1].astype(F32))
    p_flip = flip(jnp.concatenate([projector, *p_first], axis=0))
    h_other, up, down, p_flip = lax.optimization_barrier((h_other, *p_middle, p_flip))
    h_pair = jnp.concatenate([hidden, h_other], axis=0)
    h_before, h_after = shift(h_pair, "tensor", 1, 0), shift(h_pair, "tensor", -1, 0)
    p_far = shift(jnp.concatenate([up[feat:], down[feat:]], axis=0), "dp", 0, 1)
    h_before, h_after, teacher[2], p_far = lax.optimization_barrier((h_before, h_after, teacher[2], p_far))
    far_0 = shift(h_before[:own_rows], "tensor", 1, 0)
    far_1 = shift(h_after[own_rows:], "tensor", -1, 0)
    p_own = [projector, *p_first, up, down, p_far]
    p_flip = [p_flip, flip(jnp.concatenate([up, down, p_far], axis=0))]

    near = near + teacher[2].astype(F32)
    cross = lax.dynamic_index_in_dim(near, 1 - xh, 0, False).astype(BF16)
    teacher = lax.dynamic_index_in_dim(near, xh, 0, False) + shift(cross, "tensor", 0, 1).astype(F32)

    def ring_blocks(x):
        return x.reshape(-1, own_rows, hid)

    pieces = [ring_blocks(x) for x in (hidden, h_other, h_after, far_0, far_1, h_before)]
    order = (
        at
        + [((((zt + (d >> 1)) & 3) << 1) | ((d & 1) ^ xh)) for d in at]
        + [role]
    )
    order = jnp.stack([jnp.asarray(x, jnp.int32) for x in order])
    back = project(order, pieces, p_own, p_flip, teacher)
    back = lax.all_to_all(back, "tensor", 0, 0, tiled=True)
    back = jnp.sum(back.astype(F32), axis=0)
    square = join_note(back[own_rows:])
    back = back[:own_rows]

    delta = (back * sigma * (1.0 + pre * (1.0 - sigma))).astype(BF16)
    packed = flip(jnp.concatenate([delta, split_note(square, hid)], axis=0))
    delta = jnp.concatenate([delta, packed[:own_rows]], axis=0)
    square = square + join_note(packed[own_rows:])

    grad = dot(student, delta, ((0,), (0,))).astype(BF16).reshape(n_data, feat, hid)
    note = jnp.broadcast_to(split_note(square, hid)[None], (n_data, NOTE, hid))
    grad = jnp.concatenate([grad, note], axis=1)
    grad = lax.all_to_all(grad, "dp", 0, 0, tiled=True)
    grad = jnp.sum(grad.astype(F32), axis=0)
    loss = join_note(grad[feat:])[0, 0] / (2.0 * total_rows * out_width)
    return (grad[:feat] / jnp.sqrt(jnp.float32(total_rows)), loss)


def solution(mesh):
    in_specs = (
        P(None, "dp", ("role", "tensor")),
        P(("role", "tensor"), None),
        P(("role", "dp"), None),
        P(("role", "dp"), "tensor"),
        P("tensor", ("role", "dp")),
    )
    out_specs = (P(("role", "dp"), "tensor"), P())
    return jax.shard_map(shards, mesh=mesh, in_specs=in_specs, out_specs=out_specs, check_vma=False)
```

```python
import jax
import jax.numpy as jnp
from jax import lax
from jax.experimental import pallas as pl
from jax.experimental.pallas import tpu as pltpu
from jax.sharding import PartitionSpec as P

BF16 = jnp.bfloat16
F32 = jnp.float32
NOTE = 16
OFFSETS = ((0, 0), (0, 1), (1, 0), (-1, 0), (2, 0), (1, 1), (-1, 1), (2, 1))


def shift(value, axis, k, e):
    perm = [(i, ((i // 2 + k) % 4) * 2 + ((i % 2) ^ e)) for i in range(8)]
    return lax.ppermute(value, axis, perm)


def flip(value):
    return lax.ppermute(value, "role", [(0, 1), (1, 0)])


def sources(axis):
    me = lax.axis_index(axis)
    return [((((me >> 1) - k) & 3) << 1) | ((me & 1) ^ e) for k, e in OFFSETS]


def after(value, *others):
    return lax.optimization_barrier((value, *others))[0]


def gather_start(block, axis):
    return [shift(block, axis, 0, 1), shift(block, axis, 1, 0), shift(block, axis, -1, 0)]


def ring_operands(block, first):
    other, before, nxt = first
    half = block.shape[0] // 2
    return jnp.concatenate([other, before[:half]], axis=0), jnp.concatenate([other, nxt[half:]], axis=0)


def gather_middle(block, first, axis):
    up, down = ring_operands(block, first)
    return [shift(up, axis, 1, 0), shift(down, axis, -1, 0)]


def dot(a, b, dims=((1,), (0,))):
    return lax.dot_general(a, b, (dims, ((), ())), preferred_element_type=F32)


def split_note(value, width):
    value = jnp.broadcast_to(value, (1, width)).astype(F32)
    row = lax.broadcasted_iota(jnp.int32, (NOTE, width), 0)
    high = lax.reduce_precision(value, 8, 7)
    middle = lax.reduce_precision(value - high, 8, 7)
    low = value - high - middle
    note = jnp.where(row == 0, high, jnp.where(row == 1, middle, jnp.where(row == 2, low, 0.0)))
    return note.astype(BF16)


def join_note(note):
    return jnp.sum(note.astype(F32), axis=0, keepdims=True)


def project_kernel(order, *refs):
    h_refs, own_refs, other_refs = refs[:6], refs[6:13], refs[13:15]
    teacher, out, h_kept, p_kept, total, residual, h_sem, p_sem = refs[15:]
    n, width = out.shape[1] - NOTE, out.shape[2]
    size = p_kept.shape[2]
    half = size // 2
    lengths = [size] * 4 + [size + half] * 2 + [size]
    starts = [0, size, 2 * size, 3 * size, 0, size + half, 2 * (size + half)]
    other_refs = [
        other_refs[i // 4].at[pl.ds(at, length)] for i, (at, length) in enumerate(zip(starts, lengths))
    ]
    h_copies = []
    for i, (ref, at, count) in enumerate(zip(h_refs, (0, 1, 2, 4, 5, 6), (1, 1, 2, 1, 1, 2))):
        h_copies.append(pltpu.make_async_copy(ref, h_kept.at[pl.ds(at, count)], h_sem.at[i]))
    for copy in h_copies:
        copy.start()
    low, high = pl.ds(0, half), pl.ds(half, half)

    def pieces(parts):
        block, other, before, nxt, up, down, far = parts
        for whole in (block, other, before, nxt):
            yield whole.at[low], whole.at[high]
        yield up.at[pl.ds(size, half)], down.at[pl.ds(size, half)]
        for whole in (up, down, far):
            yield whole.at[low], whole.at[high]

    for j, sources_ in enumerate(zip(pieces(own_refs), pieces(other_refs))):
        for side, halves in enumerate(sources_):
            for part, source in enumerate(halves):
                target = p_kept.at[side, j, pl.ds(part * half, half)]
                pltpu.make_async_copy(source, target, p_sem.at[side, j, part]).start()

    first = order[16] == 0
    t_low, t_high = teacher[:, :width], teacher[:, width:]
    total[0] = -jnp.where(first, t_low, t_high)
    total[1] = -jnp.where(first, t_high, t_low)
    for copy in h_copies:
        copy.wait()

    @pl.loop(0, 8)
    def _(j):
        h = h_kept[order[j]]
        for side in range(2):
            for part in range(2):
                target = p_kept.at[side, j, pl.ds(part * half, half)]
                pltpu.make_async_copy(target, target, p_sem.at[side, j, part]).wait()
            total[side] += jnp.dot(h, p_kept[side, j], preferred_element_type=F32)

    squares = total[0] * total[0] + total[1] * total[1]
    value = jnp.broadcast_to(jnp.sum(squares, keepdims=True), (1, width))
    residual[...] = total[...].astype(BF16)
    row = lax.broadcasted_iota(jnp.int32, (NOTE, width), 0)
    top = value.astype(BF16).astype(F32)
    middle = (value - top).astype(BF16).astype(F32)
    bottom = value - top - middle
    note = jnp.where(row == 0, top, jnp.where(row == 1, middle, jnp.where(row == 2, bottom, 0.0)))
    note = note.astype(BF16)

    @pl.loop(0, 8)
    def _(j):
        dims = (((1,), (1,)), ((), ()))
        back = lax.dot_general(residual[0], p_kept[0, j], dims, preferred_element_type=F32)
        back += lax.dot_general(residual[1], p_kept[1, j], dims, preferred_element_type=F32)
        out[order[8 + j], :n] = back.astype(BF16)
        out[order[8 + j], n:] = note


def project(order, hidden, own, other, teacher):
    size, width = own[0].shape
    rows = teacher.shape[0]
    anywhere = pl.BlockSpec(memory_space=pl.ANY)
    inside = pl.BlockSpec(memory_space=pltpu.VMEM)
    return pl.pallas_call(
        project_kernel,
        in_specs=[pl.BlockSpec(memory_space=pltpu.SMEM)] + [anywhere] * 15 + [inside],
        out_specs=inside,
        scratch_shapes=[
            pltpu.VMEM((8, rows, size), BF16),
            pltpu.VMEM((2, 8, size, width), BF16),
            pltpu.VMEM((2, rows, width), F32),
            pltpu.VMEM((2, rows, width), BF16),
            pltpu.SemaphoreType.DMA((6,)),
            pltpu.SemaphoreType.DMA((2, 8, 2)),
        ],
        out_shape=jax.ShapeDtypeStruct((8, rows + NOTE, size), BF16),
        compiler_params=pltpu.CompilerParams(vmem_limit_bytes=32 * 1024 * 1024),
        cost_estimate=pl.CostEstimate(
            flops=64 * rows * size * width, bytes_accessed=32 * size * width, transcendentals=0
        ),
    )(order, *hidden, *own, *other, teacher)


def teach_kernel(role, tokens, weight, out, away):
    product = jnp.dot(tokens[...], weight[...], preferred_element_type=F32)
    count, rows, width = out.shape
    first = role[0] == 0
    for i in range(count):
        low, high = product[:rows, i * width : (i + 1) * width], product[rows:, i * width : (i + 1) * width]
        out[i] = jnp.where(first, low, high).astype(BF16)
        away[i] = jnp.where(first, high, low).astype(BF16)


def teach(role, teacher_in, weight, blocks, width):
    _, rows, depth = teacher_in.shape
    shape = (blocks, rows, 2 * width)
    count = 4
    steps = blocks // count
    place = pl.BlockSpec((count, rows, width), lambda j, role: (j % steps, 0, j // steps))
    return pl.pallas_call(
        teach_kernel,
        grid_spec=pltpu.PrefetchScalarGridSpec(
            num_scalar_prefetch=1,
            grid=(2 * steps,),
            in_specs=[
                pl.BlockSpec((2 * rows, depth), lambda j, role: (0, 0)),
                pl.BlockSpec((depth, count * width), lambda j, role: (0, j)),
            ],
            out_specs=[place, place],
        ),
        out_shape=[jax.ShapeDtypeStruct(shape, BF16)] * 2,
        compiler_params=pltpu.CompilerParams(
            dimension_semantics=("arbitrary",), vmem_limit_bytes=40 * 1024 * 1024
        ),
        cost_estimate=pl.CostEstimate(
            flops=8 * rows * depth * blocks * width, bytes_accessed=4 * depth * blocks * width, transcendentals=0
        ),
    )(role, teacher_in.reshape(2 * rows, depth), weight)


def shards(teacher_in, teacher_weight, student_in, student_weight, projector):
    role = lax.axis_index("role")
    n_tensor = lax.axis_size("tensor")
    n_data = lax.axis_size("dp")
    own_rows = student_in.shape[0]
    total_rows = 2 * own_rows * n_data
    out_width = teacher_weight.shape[1]
    feat, hid = student_weight.shape
    wide = feat * n_data
    cols = projector.shape[1]

    xh = lax.axis_index("tensor") & 1

    w_first = gather_start(student_weight, "dp")

    swap = []
    for d in range(8):
        for t in range(8):
            to = ((t // 2 - d // 2) % 4) * 2 + (t ^ d) % 2
            swap.append((d * 8 + t, to * 8 + d))
    projector = lax.ppermute(projector, ("dp", "tensor"), swap)

    own, away = teach(jnp.full((1,), role, jnp.int32), teacher_in, teacher_weight, n_tensor, cols)
    away, projector, *w_first = lax.optimization_barrier((away, projector, *w_first))
    away = flip(away)

    up, down = ring_operands(student_weight, w_first)
    w_middle = [shift(up, "dp", 1, 0), shift(down, "dp", -1, 0)]
    p_other = shift(projector, "dp", 0, 1)

    zt = lax.axis_index("tensor") >> 1
    teacher = {}
    for k in (0, 1, -1, 2):
        at = ((zt - k) & 3) * 2
        pair = lax.dynamic_slice_in_dim(own, at, 2, axis=0).astype(F32) + lax.dynamic_slice_in_dim(away, at, 2, axis=0).astype(F32)
        teacher[k] = pair.astype(BF16) if k == 2 else pair
    teacher = dict(zip(teacher, lax.optimization_barrier(tuple(teacher.values()))))
    over = [shift(teacher[2][0], "tensor", -1, 0), shift(teacher[2][1], "tensor", 1, 0)]

    student_in = after(student_in, teacher[2])
    mine = lax.dynamic_slice_in_dim(student_in, role * wide, wide, axis=1)
    theirs = flip(lax.dynamic_slice_in_dim(student_in, (1 - role) * wide, wide, axis=1))

    projector, p_other, theirs, *over = lax.optimization_barrier((projector, p_other, theirs, *over, *w_middle))[:5]
    teacher[1] = jnp.stack([teacher[1][0] + over[0].astype(F32), teacher[1][1]]).astype(BF16)
    teacher[-1] = jnp.stack([teacher[-1][0], teacher[-1][1] + over[1].astype(F32)]).astype(BF16)
    teacher[1], teacher[-1], student_weight = lax.optimization_barrier((teacher[1], teacher[-1], student_weight))
    for k in (1, -1):
        teacher[k] = shift(teacher[k], "tensor", -k, 0)
    up, down = w_middle
    w_far, mine, theirs = lax.optimization_barrier((jnp.concatenate([up[feat:], down[feat:]], axis=0), mine, theirs))
    w_far = shift(w_far, "dp", 0, 1)
    student = jnp.concatenate([mine, theirs], axis=0)
    p_first = [shift(projector, "dp", 1, 0), shift(projector, "dp", -1, 0)]
    w_far, *p_first = lax.optimization_barrier((w_far, *p_first))
    p_first = [p_other, *p_first]

    part = feat // 2
    at = sources("dp")
    pre = 0.0
    for j, block in enumerate((student_weight, *w_first, None, up[:feat], down[:feat], w_far)):
        columns = lax.dynamic_slice_in_dim(student, at[j] * feat, feat, axis=1)
        if block is None:
            pre = pre + dot(columns[:, :part], up[feat:]) + dot(columns[:, part:], down[feat:])
        else:
            pre = pre + dot(columns, block)
    pre = pre[:own_rows] + flip(pre[own_rows:])
    sigma = jax.nn.sigmoid(pre)
    hidden = (pre * sigma).astype(BF16)

    p_middle = gather_middle(projector, p_first, "dp")
    hidden, teacher[1], teacher[-1] = lax.optimization_barrier((hidden, teacher[1], teacher[-1]))
    h_other = shift(hidden, "tensor", 0, 1)
    near = teacher[0] + teacher[1].astype(F32) + teacher[-1].astype(F32)
    cross = lax.dynamic_index_in_dim(near, 1 - xh, 0, False).astype(BF16)
    cross = shift(cross, "tensor", 0, 1)
    p_flip = flip(jnp.concatenate([projector, *p_first], axis=0))
    h_other, up, down, p_flip = lax.optimization_barrier((h_other, *p_middle, p_flip))
    h_pair = jnp.concatenate([hidden, h_other], axis=0)
    h_before, h_after = shift(h_pair, "tensor", 1, 0), shift(h_pair, "tensor", -1, 0)
    p_far = shift(jnp.concatenate([up[feat:], down[feat:]], axis=0), "dp", 0, 1)
    h_before, h_after, p_far, cross = lax.optimization_barrier((h_before, h_after, p_far, cross))
    far_0 = shift(h_before[:own_rows], "tensor", 1, 0)
    far_1 = shift(h_after[own_rows:], "tensor", -1, 0)
    p_own = [projector, *p_first, up, down, p_far]
    p_flip = [p_flip, flip(jnp.concatenate([up, down, p_far], axis=0))]
    teacher = lax.dynamic_index_in_dim(near, xh, 0, False) + cross.astype(F32)
    hidden = [x.reshape(-1, own_rows, hid) for x in (hidden, h_other, h_after, far_0, far_1, h_before)]

    blocks = [((((zt + (d >> 1)) & 3) << 1) | ((d & 1) ^ xh)) for d in at]
    order = sources("dp") + blocks + [role]
    order = jnp.stack([jnp.asarray(x, jnp.int32) for x in order])
    back = project(order, hidden, p_own, p_flip, teacher)
    back = lax.all_to_all(back, "tensor", 0, 0, tiled=True)
    back = jnp.sum(back.astype(F32), axis=0)
    square = join_note(back[own_rows:])
    back = back[:own_rows]

    delta = (back * sigma * (1.0 + pre * (1.0 - sigma))).astype(BF16)
    packed = flip(jnp.concatenate([delta, split_note(square, hid)], axis=0))
    delta = jnp.concatenate([delta, packed[:own_rows]], axis=0)
    square = square + join_note(packed[own_rows:])

    grad = dot(student, delta, ((0,), (0,))).astype(BF16).reshape(n_data, feat, hid)
    note = jnp.broadcast_to(split_note(square, hid)[None], (n_data, NOTE, hid))
    grad = jnp.concatenate([grad, note], axis=1)
    grad = lax.all_to_all(grad, "dp", 0, 0, tiled=True)
    grad = jnp.sum(grad.astype(F32), axis=0)
    loss = join_note(grad[feat:])[0, 0] / (2.0 * total_rows * out_width)
    return (grad[:feat] / jnp.sqrt(jnp.float32(total_rows)), loss)


def solution(mesh):
    in_specs = (
        P(None, "dp", ("role", "tensor")),
        P(("role", "tensor"), None),
        P(("role", "dp"), None),
        P(("role", "dp"), "tensor"),
        P("tensor", ("role", "dp")),
    )
    out_specs = (P(("role", "dp"), "tensor"), P())
    return jax.shard_map(shards, mesh=mesh, in_specs=in_specs, out_specs=out_specs, check_vma=False)
```

```python
import jax
import jax.numpy as jnp
from jax import lax
from jax.experimental import pallas as pl
from jax.experimental.pallas import tpu as pltpu
from jax.sharding import PartitionSpec as P

BF16 = jnp.bfloat16
F32 = jnp.float32
NOTE = 16
OFFSETS = ((0, 0), (0, 1), (1, 0), (-1, 0), (2, 0), (1, 1), (-1, 1), (2, 1))


def shift(value, axis, k, e):
    perm = [(i, ((i // 2 + k) % 4) * 2 + ((i % 2) ^ e)) for i in range(8)]
    return lax.ppermute(value, axis, perm)


def flip(value):
    return lax.ppermute(value, "role", [(0, 1), (1, 0)])


def sources(axis):
    me = lax.axis_index(axis)
    return [((((me >> 1) - k) & 3) << 1) | ((me & 1) ^ e) for k, e in OFFSETS]


def after(value, *others):
    return lax.optimization_barrier((value, *others))[0]


def gather_start(block, axis):
    return [shift(block, axis, 0, 1), shift(block, axis, 1, 0), shift(block, axis, -1, 0)]


def ring_operands(block, first):
    other, before, nxt = first
    half = block.shape[0] // 2
    return jnp.concatenate([other, before[:half]], axis=0), jnp.concatenate([other, nxt[half:]], axis=0)


def gather_middle(block, first, axis):
    up, down = ring_operands(block, first)
    return [shift(up, axis, 1, 0), shift(down, axis, -1, 0)]


def dot(a, b, dims=((1,), (0,))):
    return lax.dot_general(a, b, (dims, ((), ())), preferred_element_type=F32)


def split_note(value, width):
    value = jnp.broadcast_to(value, (1, width)).astype(F32)
    row = lax.broadcasted_iota(jnp.int32, (NOTE, width), 0)
    high = lax.reduce_precision(value, 8, 7)
    middle = lax.reduce_precision(value - high, 8, 7)
    low = value - high - middle
    note = jnp.where(row == 0, high, jnp.where(row == 1, middle, jnp.where(row == 2, low, 0.0)))
    return note.astype(BF16)


def join_note(note):
    return jnp.sum(note.astype(F32), axis=0, keepdims=True)


def project_kernel(order, *refs):
    h_refs, own_refs, other_refs = refs[:6], refs[6:13], refs[13:15]
    teacher, out, h_kept, p_kept, total, residual, h_sem, p_sem = refs[15:]
    n, width = out.shape[1] - NOTE, out.shape[2]
    size = p_kept.shape[2]
    half = size // 2
    lengths = [size] * 4 + [size + half] * 2 + [size]
    starts = [0, size, 2 * size, 3 * size, 0, size + half, 2 * (size + half)]
    other_refs = [
        other_refs[i // 4].at[pl.ds(at, length)] for i, (at, length) in enumerate(zip(starts, lengths))
    ]
    h_copies = []
    for i, (ref, at, count) in enumerate(zip(h_refs, (0, 1, 2, 4, 5, 6), (1, 1, 2, 1, 1, 2))):
        h_copies.append(pltpu.make_async_copy(ref, h_kept.at[pl.ds(at, count)], h_sem.at[i]))
    for copy in h_copies:
        copy.start()
    low, high = pl.ds(0, half), pl.ds(half, half)

    def pieces(parts):
        block, other, before, nxt, up, down, far = parts
        for whole in (block, other, before, nxt):
            yield whole.at[low], whole.at[high]
        yield up.at[pl.ds(size, half)], down.at[pl.ds(size, half)]
        for whole in (up, down, far):
            yield whole.at[low], whole.at[high]

    for j, sources_ in enumerate(zip(pieces(own_refs), pieces(other_refs))):
        for side, halves in enumerate(sources_):
            for part, source in enumerate(halves):
                target = p_kept.at[side, j, pl.ds(part * half, half)]
                pltpu.make_async_copy(source, target, p_sem.at[side, j, part]).start()

    first = order[16] == 0
    t_low, t_high = teacher[:, :width], teacher[:, width:]
    total[0] = -jnp.where(first, t_low, t_high)
    total[1] = -jnp.where(first, t_high, t_low)
    for copy in h_copies:
        copy.wait()

    @pl.loop(0, 8)
    def _(j):
        h = h_kept[order[j]]
        for side in range(2):
            for part in range(2):
                target = p_kept.at[side, j, pl.ds(part * half, half)]
                pltpu.make_async_copy(target, target, p_sem.at[side, j, part]).wait()
            total[side] += jnp.dot(h, p_kept[side, j], preferred_element_type=F32)

    squares = total[0] * total[0] + total[1] * total[1]
    value = jnp.broadcast_to(jnp.sum(squares, keepdims=True), (1, width))
    residual[...] = total[...].astype(BF16)
    row = lax.broadcasted_iota(jnp.int32, (NOTE, width), 0)
    top = value.astype(BF16).astype(F32)
    middle = (value - top).astype(BF16).astype(F32)
    bottom = value - top - middle
    note = jnp.where(row == 0, top, jnp.where(row == 1, middle, jnp.where(row == 2, bottom, 0.0)))
    note = note.astype(BF16)

    @pl.loop(0, 8)
    def _(j):
        dims = (((1,), (1,)), ((), ()))
        back = lax.dot_general(residual[0], p_kept[0, j], dims, preferred_element_type=F32)
        back += lax.dot_general(residual[1], p_kept[1, j], dims, preferred_element_type=F32)
        out[order[8 + j], :n] = back.astype(BF16)
        out[order[8 + j], n:] = note


def project(order, hidden, own, other, teacher):
    size, width = own[0].shape
    rows = teacher.shape[0]
    anywhere = pl.BlockSpec(memory_space=pl.ANY)
    inside = pl.BlockSpec(memory_space=pltpu.VMEM)
    return pl.pallas_call(
        project_kernel,
        in_specs=[pl.BlockSpec(memory_space=pltpu.SMEM)] + [anywhere] * 15 + [inside],
        out_specs=inside,
        scratch_shapes=[
            pltpu.VMEM((8, rows, size), BF16),
            pltpu.VMEM((2, 8, size, width), BF16),
            pltpu.VMEM((2, rows, width), F32),
            pltpu.VMEM((2, rows, width), BF16),
            pltpu.SemaphoreType.DMA((6,)),
            pltpu.SemaphoreType.DMA((2, 8, 2)),
        ],
        out_shape=jax.ShapeDtypeStruct((8, rows + NOTE, size), BF16),
        compiler_params=pltpu.CompilerParams(vmem_limit_bytes=32 * 1024 * 1024),
        cost_estimate=pl.CostEstimate(
            flops=64 * rows * size * width, bytes_accessed=32 * size * width, transcendentals=0
        ),
    )(order, *hidden, *own, *other, teacher)


def teach_kernel(role, tokens, weight, out, away):
    product = jnp.dot(tokens[...], weight[...], preferred_element_type=F32)
    count, rows, width = out.shape
    first = role[0] == 0
    for i in range(count):
        low, high = product[:rows, i * width : (i + 1) * width], product[rows:, i * width : (i + 1) * width]
        out[i] = jnp.where(first, low, high).astype(BF16)
        away[i] = jnp.where(first, high, low).astype(BF16)


def teach(role, teacher_in, weight, blocks, width):
    _, rows, depth = teacher_in.shape
    shape = (blocks, rows, 2 * width)
    count = 4
    steps = blocks // count
    place = pl.BlockSpec((count, rows, width), lambda j, role: (j % steps, 0, j // steps))
    return pl.pallas_call(
        teach_kernel,
        grid_spec=pltpu.PrefetchScalarGridSpec(
            num_scalar_prefetch=1,
            grid=(2 * steps,),
            in_specs=[
                pl.BlockSpec((2 * rows, depth), lambda j, role: (0, 0)),
                pl.BlockSpec((depth, count * width), lambda j, role: (0, j)),
            ],
            out_specs=[place, place],
        ),
        out_shape=[jax.ShapeDtypeStruct(shape, BF16)] * 2,
        compiler_params=pltpu.CompilerParams(
            dimension_semantics=("arbitrary",), vmem_limit_bytes=40 * 1024 * 1024
        ),
        cost_estimate=pl.CostEstimate(
            flops=8 * rows * depth * blocks * width, bytes_accessed=4 * depth * blocks * width, transcendentals=0
        ),
    )(role, teacher_in.reshape(2 * rows, depth), weight)


def shards(teacher_in, teacher_weight, student_in, student_weight, projector):
    role = lax.axis_index("role")
    n_tensor = lax.axis_size("tensor")
    n_data = lax.axis_size("dp")
    own_rows = student_in.shape[0]
    total_rows = 2 * own_rows * n_data
    out_width = teacher_weight.shape[1]
    feat, hid = student_weight.shape
    wide = feat * n_data
    cols = projector.shape[1]

    xh = lax.axis_index("tensor") & 1

    w_first = gather_start(student_weight, "dp")

    swap = []
    for d in range(8):
        for t in range(8):
            to = ((t // 2 - d // 2) % 4) * 2 + (t ^ d) % 2
            swap.append((d * 8 + t, to * 8 + d))
    projector = lax.ppermute(projector, ("dp", "tensor"), swap)

    mine = lax.dynamic_slice_in_dim(student_in, role * wide, wide, axis=1)
    theirs = lax.dynamic_slice_in_dim(student_in, (1 - role) * wide, wide, axis=1)
    mine, theirs = lax.optimization_barrier((mine, theirs))
    theirs = flip(theirs)

    own, away = teach(jnp.full((1,), role, jnp.int32), teacher_in, teacher_weight, n_tensor, cols)
    away, projector, theirs, *w_first = lax.optimization_barrier((away, projector, theirs, *w_first))
    away = flip(away)

    up, down = ring_operands(student_weight, w_first)
    w_middle = [shift(up, "dp", 1, 0), shift(down, "dp", -1, 0)]
    p_other = shift(projector, "dp", 0, 1)

    zt = lax.axis_index("tensor") >> 1
    teacher = {}
    for k in (0, 1, -1, 2):
        at = ((zt - k) & 3) * 2
        pair = lax.dynamic_slice_in_dim(own, at, 2, axis=0).astype(F32) + lax.dynamic_slice_in_dim(away, at, 2, axis=0).astype(F32)
        teacher[k] = pair.astype(BF16) if k == 2 else pair
    teacher = dict(zip(teacher, lax.optimization_barrier(tuple(teacher.values()))))
    over = [shift(teacher[2][0], "tensor", -1, 0), shift(teacher[2][1], "tensor", 1, 0)]

    projector, p_other, *moved = lax.optimization_barrier((projector, p_other, *over, *w_middle))
    over, w_middle = moved[:2], moved[2:]
    teacher[1] = (teacher[1] + jnp.pad(over[0][None].astype(F32), ((0, 1), (0, 0), (0, 0)))).astype(BF16)
    teacher[-1] = (teacher[-1] + jnp.pad(over[1][None].astype(F32), ((1, 0), (0, 0), (0, 0)))).astype(BF16)
    teacher[1], teacher[-1], student_weight = lax.optimization_barrier((teacher[1], teacher[-1], student_weight))
    for k in (1, -1):
        teacher[k] = shift(teacher[k], "tensor", -k, 0)
    up, down = w_middle
    w_far, mine, theirs = lax.optimization_barrier((jnp.concatenate([up[feat:], down[feat:]], axis=0), mine, theirs))
    w_far = shift(w_far, "dp", 0, 1)
    student = jnp.concatenate([mine, theirs], axis=0)
    p_first = [shift(projector, "dp", 1, 0), shift(projector, "dp", -1, 0)]
    w_far, *p_first = lax.optimization_barrier((w_far, *p_first))
    p_first = [p_other, *p_first]

    part = feat // 2
    at = sources("dp")
    pre = 0.0
    for j, block in enumerate((student_weight, *w_first, None, up[:feat], down[:feat], w_far)):
        columns = lax.dynamic_slice_in_dim(student, at[j] * feat, feat, axis=1)
        if block is None:
            pre = pre + dot(columns[:, :part], up[feat:]) + dot(columns[:, part:], down[feat:])
        else:
            pre = pre + dot(columns, block)
    pre = pre[:own_rows] + flip(pre[own_rows:])
    sigma = jax.nn.sigmoid(pre)
    hidden = (pre * sigma).astype(BF16)

    p_middle = gather_middle(projector, p_first, "dp")
    hidden, teacher[1], teacher[-1] = lax.optimization_barrier((hidden, teacher[1], teacher[-1]))
    h_other = shift(hidden, "tensor", 0, 1)
    near = teacher[0] + teacher[1].astype(F32) + teacher[-1].astype(F32)
    cross = lax.dynamic_index_in_dim(near, 1 - xh, 0, False).astype(BF16)
    cross = shift(cross, "tensor", 0, 1)
    p_flip = flip(jnp.concatenate([projector, *p_first], axis=0))
    h_other, up, down, p_flip = lax.optimization_barrier((h_other, *p_middle, p_flip))
    h_pair = jnp.concatenate([hidden, h_other], axis=0)
    h_before, h_after = shift(h_pair, "tensor", 1, 0), shift(h_pair, "tensor", -1, 0)
    p_far = shift(jnp.concatenate([up[feat:], down[feat:]], axis=0), "dp", 0, 1)
    h_before, h_after, p_far, cross = lax.optimization_barrier((h_before, h_after, p_far, cross))
    far_0 = shift(h_before[:own_rows], "tensor", 1, 0)
    far_1 = shift(h_after[own_rows:], "tensor", -1, 0)
    p_own = [projector, *p_first, up, down, p_far]
    p_flip = [p_flip, flip(jnp.concatenate([up, down, p_far], axis=0))]
    teacher = lax.dynamic_index_in_dim(near, xh, 0, False) + cross.astype(F32)
    hidden = [x.reshape(-1, own_rows, hid) for x in (hidden, h_other, h_after, far_0, far_1, h_before)]

    blocks = [((((zt + (d >> 1)) & 3) << 1) | ((d & 1) ^ xh)) for d in at]
    order = sources("dp") + blocks + [role]
    order = jnp.stack([jnp.asarray(x, jnp.int32) for x in order])
    back = project(order, hidden, p_own, p_flip, teacher)
    back = lax.all_to_all(back, "tensor", 0, 0, tiled=True)
    back = jnp.sum(back.astype(F32), axis=0)
    square = join_note(back[own_rows:])
    back = back[:own_rows]

    delta = (back * sigma * (1.0 + pre * (1.0 - sigma))).astype(BF16)
    packed = flip(jnp.concatenate([delta, split_note(square, hid)], axis=0))
    delta = jnp.concatenate([delta, packed[:own_rows]], axis=0)
    square = square + join_note(packed[own_rows:])

    grad = dot(student, delta, ((0,), (0,))).astype(BF16).reshape(n_data, feat, hid)
    note = jnp.broadcast_to(split_note(square, hid)[None], (n_data, NOTE, hid))
    grad = jnp.concatenate([grad, note], axis=1)
    grad = lax.all_to_all(grad, "dp", 0, 0, tiled=True)
    grad = jnp.sum(grad.astype(F32), axis=0)
    loss = join_note(grad[feat:])[0, 0] / (2.0 * total_rows * out_width)
    return (grad[:feat] / jnp.sqrt(jnp.float32(total_rows)), loss)


def solution(mesh):
    in_specs = (
        P(None, "dp", ("role", "tensor")),
        P(("role", "tensor"), None),
        P(("role", "dp"), None),
        P(("role", "dp"), "tensor"),
        P("tensor", ("role", "dp")),
    )
    out_specs = (P(("role", "dp"), "tensor"), P())
    return jax.shard_map(shards, mesh=mesh, in_specs=in_specs, out_specs=out_specs, check_vma=False)
```

```python
import jax
import jax.numpy as jnp
from jax import lax
from jax.experimental import pallas as pl
from jax.experimental.pallas import tpu as pltpu
from jax.sharding import PartitionSpec as P

BF16 = jnp.bfloat16
F32 = jnp.float32
NOTE = 16
OFFSETS = ((0, 0), (0, 1), (1, 0), (-1, 0), (2, 0), (1, 1), (-1, 1), (2, 1))


def shift(value, axis, k, e):
    perm = [(i, ((i // 2 + k) % 4) * 2 + ((i % 2) ^ e)) for i in range(8)]
    return lax.ppermute(value, axis, perm)


def flip(value):
    return lax.ppermute(value, "role", [(0, 1), (1, 0)])


def sources(axis):
    me = lax.axis_index(axis)
    return [((((me >> 1) - k) & 3) << 1) | ((me & 1) ^ e) for k, e in OFFSETS]


def after(value, *others):
    return lax.optimization_barrier((value, *others))[0]


def gather_start(block, axis):
    return [shift(block, axis, 0, 1), shift(block, axis, 1, 0), shift(block, axis, -1, 0)]


def ring_operands(block, first):
    other, before, nxt = first
    half = block.shape[0] // 2
    return jnp.concatenate([other, before[:half]], axis=0), jnp.concatenate([other, nxt[half:]], axis=0)


def gather_middle(block, first, axis):
    up, down = ring_operands(block, first)
    return [shift(up, axis, 1, 0), shift(down, axis, -1, 0)]


def dot(a, b, dims=((1,), (0,))):
    return lax.dot_general(a, b, (dims, ((), ())), preferred_element_type=F32)


def split_note(value, width):
    value = jnp.broadcast_to(value, (1, width)).astype(F32)
    row = lax.broadcasted_iota(jnp.int32, (NOTE, width), 0)
    high = lax.reduce_precision(value, 8, 7)
    middle = lax.reduce_precision(value - high, 8, 7)
    low = value - high - middle
    note = jnp.where(row == 0, high, jnp.where(row == 1, middle, jnp.where(row == 2, low, 0.0)))
    return note.astype(BF16)


def join_note(note):
    return jnp.sum(note.astype(F32), axis=0, keepdims=True)


def project_kernel(order, *refs):
    h_refs, own_refs, other_refs = refs[:6], refs[6:14], refs[14:16]
    teacher, out, h_kept, p_kept, total, residual, h_sem, p_sem = refs[16:]
    n, width = out.shape[1] - NOTE, out.shape[2]
    size = p_kept.shape[2]
    half = size // 2
    lengths = [size] * 4 + [size + half] * 2 + [half] * 2
    starts = [0, size, 2 * size, 3 * size, 0, size + half, 2 * (size + half), 3 * size + half]
    other_refs = [
        other_refs[i // 4].at[pl.ds(at, length)] for i, (at, length) in enumerate(zip(starts, lengths))
    ]
    h_copies = []
    for i, (ref, at, count) in enumerate(zip(h_refs, (0, 1, 2, 4, 5, 6), (1, 1, 2, 1, 1, 2))):
        h_copies.append(pltpu.make_async_copy(ref, h_kept.at[pl.ds(at, count)], h_sem.at[i]))
    for copy in h_copies:
        copy.start()
    low, high = pl.ds(0, half), pl.ds(half, half)

    def pieces(parts):
        block, other, before, nxt, up, down, *far = parts
        for whole in (block, other, before, nxt):
            yield whole.at[low], whole.at[high]
        yield up.at[pl.ds(size, half)], down.at[pl.ds(size, half)]
        for whole in (up, down):
            yield whole.at[low], whole.at[high]
        yield far[0].at[low], far[1].at[low]

    for j, sources_ in enumerate(zip(pieces(own_refs), pieces(other_refs))):
        for side, halves in enumerate(sources_):
            for part, source in enumerate(halves):
                target = p_kept.at[side, j, pl.ds(part * half, half)]
                pltpu.make_async_copy(source, target, p_sem.at[side, j, part]).start()

    first = order[16] == 0
    t_low, t_high = teacher[:, :width], teacher[:, width:]
    total[0] = -jnp.where(first, t_low, t_high)
    total[1] = -jnp.where(first, t_high, t_low)
    for copy in h_copies:
        copy.wait()

    @pl.loop(0, 8)
    def _(j):
        h = h_kept[order[j]]
        for side in range(2):
            for part in range(2):
                target = p_kept.at[side, j, pl.ds(part * half, half)]
                pltpu.make_async_copy(target, target, p_sem.at[side, j, part]).wait()
            total[side] += jnp.dot(h, p_kept[side, j], preferred_element_type=F32)

    squares = total[0] * total[0] + total[1] * total[1]
    value = jnp.broadcast_to(jnp.sum(squares, keepdims=True), (1, width))
    residual[...] = total[...].astype(BF16)
    row = lax.broadcasted_iota(jnp.int32, (NOTE, width), 0)
    top = value.astype(BF16).astype(F32)
    middle = (value - top).astype(BF16).astype(F32)
    bottom = value - top - middle
    note = jnp.where(row == 0, top, jnp.where(row == 1, middle, jnp.where(row == 2, bottom, 0.0)))
    note = note.astype(BF16)

    @pl.loop(0, 8)
    def _(j):
        dims = (((1,), (1,)), ((), ()))
        back = lax.dot_general(residual[0], p_kept[0, j], dims, preferred_element_type=F32)
        back += lax.dot_general(residual[1], p_kept[1, j], dims, preferred_element_type=F32)
        out[order[8 + j], :n] = back.astype(BF16)
        out[order[8 + j], n:] = note


def project(order, hidden, own, other, teacher):
    size, width = own[0].shape
    rows = teacher.shape[0]
    anywhere = pl.BlockSpec(memory_space=pl.ANY)
    inside = pl.BlockSpec(memory_space=pltpu.VMEM)
    return pl.pallas_call(
        project_kernel,
        in_specs=[pl.BlockSpec(memory_space=pltpu.SMEM)] + [anywhere] * 16 + [inside],
        out_specs=inside,
        scratch_shapes=[
            pltpu.VMEM((8, rows, size), BF16),
            pltpu.VMEM((2, 8, size, width), BF16),
            pltpu.VMEM((2, rows, width), F32),
            pltpu.VMEM((2, rows, width), BF16),
            pltpu.SemaphoreType.DMA((6,)),
            pltpu.SemaphoreType.DMA((2, 8, 2)),
        ],
        out_shape=jax.ShapeDtypeStruct((8, rows + NOTE, size), BF16),
        compiler_params=pltpu.CompilerParams(vmem_limit_bytes=32 * 1024 * 1024),
        cost_estimate=pl.CostEstimate(
            flops=64 * rows * size * width, bytes_accessed=32 * size * width, transcendentals=0
        ),
    )(order, *hidden, *own, *other, teacher)


def teach_kernel(role, tokens, weight, out, away):
    product = jnp.dot(tokens[...], weight[...], preferred_element_type=F32)
    count, rows, width = out.shape
    first = role[0] == 0
    for i in range(count):
        low, high = product[:rows, i * width : (i + 1) * width], product[rows:, i * width : (i + 1) * width]
        out[i] = jnp.where(first, low, high).astype(BF16)
        away[i] = jnp.where(first, high, low).astype(BF16)


def teach(role, teacher_in, weight, blocks, width):
    _, rows, depth = teacher_in.shape
    shape = (blocks, rows, 2 * width)
    count = 4
    steps = blocks // count
    place = pl.BlockSpec((count, rows, width), lambda j, role: (j % steps, 0, j // steps))
    return pl.pallas_call(
        teach_kernel,
        grid_spec=pltpu.PrefetchScalarGridSpec(
            num_scalar_prefetch=1,
            grid=(2 * steps,),
            in_specs=[
                pl.BlockSpec((2 * rows, depth), lambda j, role: (0, 0)),
                pl.BlockSpec((depth, count * width), lambda j, role: (0, j)),
            ],
            out_specs=[place, place],
        ),
        out_shape=[jax.ShapeDtypeStruct(shape, BF16)] * 2,
        compiler_params=pltpu.CompilerParams(
            dimension_semantics=("arbitrary",), vmem_limit_bytes=40 * 1024 * 1024
        ),
        cost_estimate=pl.CostEstimate(
            flops=8 * rows * depth * blocks * width, bytes_accessed=4 * depth * blocks * width, transcendentals=0
        ),
    )(role, teacher_in.reshape(2 * rows, depth), weight)


def shards(teacher_in, teacher_weight, student_in, student_weight, projector):
    role = lax.axis_index("role")
    n_tensor = lax.axis_size("tensor")
    n_data = lax.axis_size("dp")
    own_rows = student_in.shape[0]
    total_rows = 2 * own_rows * n_data
    out_width = teacher_weight.shape[1]
    feat, hid = student_weight.shape
    wide = feat * n_data
    cols = projector.shape[1]

    xh = lax.axis_index("tensor") & 1

    w_first = gather_start(student_weight, "dp")

    swap = []
    for d in range(8):
        for t in range(8):
            to = ((t // 2 - d // 2) % 4) * 2 + (t ^ d) % 2
            swap.append((d * 8 + t, to * 8 + d))
    projector = lax.ppermute(projector, ("dp", "tensor"), swap)

    mine = lax.dynamic_slice_in_dim(student_in, role * wide, wide, axis=1)
    theirs = lax.dynamic_slice_in_dim(student_in, (1 - role) * wide, wide, axis=1)
    mine, theirs = lax.optimization_barrier((mine, theirs))
    theirs = flip(theirs)

    own, away = teach(jnp.full((1,), role, jnp.int32), teacher_in, teacher_weight, n_tensor, cols)
    away, projector, theirs, *w_first = lax.optimization_barrier((away, projector, theirs, *w_first))
    away = flip(away)

    up, down = ring_operands(student_weight, w_first)
    w_middle = [shift(up, "dp", 1, 0), shift(down, "dp", -1, 0)]
    p_other = shift(projector, "dp", 0, 1)

    zt = lax.axis_index("tensor") >> 1
    teacher = {}
    for k in (0, 1, -1, 2):
        at = ((zt - k) & 3) * 2
        pair = lax.dynamic_slice_in_dim(own, at, 2, axis=0).astype(F32) + lax.dynamic_slice_in_dim(away, at, 2, axis=0).astype(F32)
        teacher[k] = pair.astype(BF16) if k == 2 else pair
    teacher = dict(zip(teacher, lax.optimization_barrier(tuple(teacher.values()))))
    over = [shift(teacher[2][0], "tensor", -1, 0), shift(teacher[2][1], "tensor", 1, 0)]

    projector, p_other, *moved = lax.optimization_barrier((projector, p_other, *over, *w_middle))
    over, w_middle = moved[:2], moved[2:]
    teacher[1] = (teacher[1] + jnp.pad(over[0][None].astype(F32), ((0, 1), (0, 0), (0, 0)))).astype(BF16)
    teacher[-1] = (teacher[-1] + jnp.pad(over[1][None].astype(F32), ((1, 0), (0, 0), (0, 0)))).astype(BF16)
    teacher[1], teacher[-1], student_weight = lax.optimization_barrier((teacher[1], teacher[-1], student_weight))
    for k in (1, -1):
        teacher[k] = shift(teacher[k], "tensor", -k, 0)
    up, down = w_middle
    w_far, mine, theirs = lax.optimization_barrier((jnp.concatenate([up[feat:], down[feat:]], axis=0), mine, theirs))
    w_far = shift(w_far, "dp", 0, 1)
    student = jnp.concatenate([mine, theirs], axis=0)
    p_first = [shift(projector, "dp", 1, 0), shift(projector, "dp", -1, 0)]
    w_far, *p_first = lax.optimization_barrier((w_far, *p_first))
    p_first = [p_other, *p_first]

    part = feat // 2
    at = sources("dp")
    pre = 0.0
    for j, block in enumerate((student_weight, *w_first, None, up[:feat], down[:feat], w_far)):
        columns = lax.dynamic_slice_in_dim(student, at[j] * feat, feat, axis=1)
        if block is None:
            pre = pre + dot(columns[:, :part], up[feat:]) + dot(columns[:, part:], down[feat:])
        else:
            pre = pre + dot(columns, block)
    pre = pre[:own_rows] + flip(pre[own_rows:])
    sigma = jax.nn.sigmoid(pre)
    hidden = (pre * sigma).astype(BF16)

    p_middle = gather_middle(projector, p_first, "dp")
    h_other = shift(hidden, "tensor", 0, 1)
    h_other, up, down, teacher[1], teacher[-1] = lax.optimization_barrier(
        (h_other, *p_middle, teacher[1], teacher[-1])
    )
    p_flip = flip(jnp.concatenate([after(projector, h_other), *p_first], axis=0))
    near = teacher[0] + teacher[1].astype(F32) + teacher[-1].astype(F32)
    cross = lax.dynamic_index_in_dim(near, 1 - xh, 0, False).astype(BF16)
    cross = shift(cross, "tensor", 0, 1)
    h_pair = jnp.concatenate([hidden, h_other], axis=0)
    h_before, h_after = shift(h_pair, "tensor", 1, 0), shift(h_pair, "tensor", -1, 0)
    p_far = [shift(up[:part], "dp", 1, 0), shift(down[part:feat], "dp", -1, 0)]
    h_before, h_after, cross, *p_far = lax.optimization_barrier((h_before, h_after, cross, *p_far))
    far_0 = shift(h_before[:own_rows], "tensor", 1, 0)
    far_1 = shift(h_after[own_rows:], "tensor", -1, 0)
    p_own = [projector, *p_first, up, down, *p_far]
    p_flip = [p_flip, flip(jnp.concatenate([up, down, *p_far], axis=0))]
    teacher = lax.dynamic_index_in_dim(near, xh, 0, False) + cross.astype(F32)
    hidden = [x.reshape(-1, own_rows, hid) for x in (hidden, h_other, h_after, far_0, far_1, h_before)]

    blocks = [((((zt + (d >> 1)) & 3) << 1) | ((d & 1) ^ xh)) for d in at]
    order = sources("dp") + blocks + [role]
    order = jnp.stack([jnp.asarray(x, jnp.int32) for x in order])
    back = project(order, hidden, p_own, p_flip, teacher)
    back = lax.all_to_all(back, "tensor", 0, 0, tiled=True)
    back = jnp.sum(back.astype(F32), axis=0)
    square = join_note(back[own_rows:])
    back = back[:own_rows]

    delta = (back * sigma * (1.0 + pre * (1.0 - sigma))).astype(BF16)
    packed = flip(jnp.concatenate([delta, split_note(square, hid)], axis=0))
    delta = jnp.concatenate([delta, packed[:own_rows]], axis=0)
    square = square + join_note(packed[own_rows:])

    grad = dot(student, delta, ((0,), (0,))).astype(BF16).reshape(n_data, feat, hid)
    note = jnp.broadcast_to(split_note(square, hid)[None], (n_data, NOTE, hid))
    grad = jnp.concatenate([grad, note], axis=1)
    grad = lax.all_to_all(grad, "dp", 0, 0, tiled=True)
    grad = jnp.sum(grad.astype(F32), axis=0)
    loss = join_note(grad[feat:])[0, 0] / (2.0 * total_rows * out_width)
    return (grad[:feat] / jnp.sqrt(jnp.float32(total_rows)), loss)


def solution(mesh):
    in_specs = (
        P(None, "dp", ("role", "tensor")),
        P(("role", "tensor"), None),
        P(("role", "dp"), None),
        P(("role", "dp"), "tensor"),
        P("tensor", ("role", "dp")),
    )
    out_specs = (P(("role", "dp"), "tensor"), P())
    return jax.shard_map(shards, mesh=mesh, in_specs=in_specs, out_specs=out_specs, check_vma=False)
```

```python
import jax
import jax.numpy as jnp
from jax import lax
from jax.experimental import pallas as pl
from jax.experimental.pallas import tpu as pltpu
from jax.sharding import PartitionSpec as P

BF16 = jnp.bfloat16
F32 = jnp.float32
NOTE = 16
OFFSETS = ((0, 0), (0, 1), (1, 0), (-1, 0), (2, 0), (1, 1), (-1, 1), (2, 1))


def shift(value, axis, k, e):
    perm = [(i, ((i // 2 + k) % 4) * 2 + ((i % 2) ^ e)) for i in range(8)]
    return lax.ppermute(value, axis, perm)


def flip(value):
    return lax.ppermute(value, "role", [(0, 1), (1, 0)])


def sources(axis):
    me = lax.axis_index(axis)
    return [((((me >> 1) - k) & 3) << 1) | ((me & 1) ^ e) for k, e in OFFSETS]


def after(value, *others):
    return lax.optimization_barrier((value, *others))[0]


def gather_start(block, axis):
    return [shift(block, axis, 0, 1), shift(block, axis, 1, 0), shift(block, axis, -1, 0)]


def ring_operands(block, first):
    other, before, nxt = first
    half = block.shape[0] // 2
    return jnp.concatenate([other, before[:half]], axis=0), jnp.concatenate([other, nxt[half:]], axis=0)


def gather_middle(block, first, axis):
    up, down = ring_operands(block, first)
    return [shift(up, axis, 1, 0), shift(down, axis, -1, 0)]


def dot(a, b, dims=((1,), (0,))):
    return lax.dot_general(a, b, (dims, ((), ())), preferred_element_type=F32)


def split_note(value, width):
    value = jnp.broadcast_to(value, (1, width)).astype(F32)
    row = lax.broadcasted_iota(jnp.int32, (NOTE, width), 0)
    high = lax.reduce_precision(value, 8, 7)
    middle = lax.reduce_precision(value - high, 8, 7)
    low = value - high - middle
    note = jnp.where(row == 0, high, jnp.where(row == 1, middle, jnp.where(row == 2, low, 0.0)))
    return note.astype(BF16)


def join_note(note):
    return jnp.sum(note.astype(F32), axis=0, keepdims=True)


def project_kernel(order, *refs):
    h_refs, own_refs, other_refs = refs[:6], refs[6:14], refs[14:16]
    teacher, out, h_kept, p_kept, total, residual, h_sem, p_sem = refs[16:]
    n, width = out.shape[1] - NOTE, out.shape[2]
    size = p_kept.shape[2]
    half = size // 2
    lengths = [size] * 4 + [size + half] * 2 + [half] * 2
    starts = [0, size, 2 * size, 3 * size, 0, size + half, 2 * (size + half), 3 * size + half]
    other_refs = [
        other_refs[i // 4].at[pl.ds(at, length)] for i, (at, length) in enumerate(zip(starts, lengths))
    ]
    h_copies = []
    for i, (ref, at, count) in enumerate(zip(h_refs, (0, 1, 2, 4, 5, 6), (1, 1, 2, 1, 1, 2))):
        h_copies.append(pltpu.make_async_copy(ref, h_kept.at[pl.ds(at, count)], h_sem.at[i]))
    for copy in h_copies:
        copy.start()
    low, high = pl.ds(0, half), pl.ds(half, half)

    def pieces(parts):
        block, other, before, nxt, up, down, *far = parts
        for whole in (block, other, before, nxt):
            yield whole.at[low], whole.at[high]
        yield up.at[pl.ds(size, half)], down.at[pl.ds(size, half)]
        for whole in (up, down):
            yield whole.at[low], whole.at[high]
        yield far[0].at[low], far[1].at[low]

    for j, sources_ in enumerate(zip(pieces(own_refs), pieces(other_refs))):
        for side, halves in enumerate(sources_):
            for part, source in enumerate(halves):
                target = p_kept.at[side, j, pl.ds(part * half, half)]
                pltpu.make_async_copy(source, target, p_sem.at[side, j, part]).start()

    first = order[16] == 0
    t_low, t_high = teacher[:, :width], teacher[:, width:]
    total[0] = -jnp.where(first, t_low, t_high)
    total[1] = -jnp.where(first, t_high, t_low)
    for copy in h_copies:
        copy.wait()

    @pl.loop(0, 8)
    def _(j):
        h = h_kept[order[j]]
        for side in range(2):
            for part in range(2):
                target = p_kept.at[side, j, pl.ds(part * half, half)]
                pltpu.make_async_copy(target, target, p_sem.at[side, j, part]).wait()
            total[side] += jnp.dot(h, p_kept[side, j], preferred_element_type=F32)

    squares = total[0] * total[0] + total[1] * total[1]
    value = jnp.broadcast_to(jnp.sum(squares, keepdims=True), (1, width))
    residual[...] = total[...].astype(BF16)
    row = lax.broadcasted_iota(jnp.int32, (NOTE, width), 0)
    top = value.astype(BF16).astype(F32)
    middle = (value - top).astype(BF16).astype(F32)
    bottom = value - top - middle
    note = jnp.where(row == 0, top, jnp.where(row == 1, middle, jnp.where(row == 2, bottom, 0.0)))
    note = note.astype(BF16)

    @pl.loop(0, 8)
    def _(j):
        dims = (((1,), (1,)), ((), ()))
        back = lax.dot_general(residual[0], p_kept[0, j], dims, preferred_element_type=F32)
        back += lax.dot_general(residual[1], p_kept[1, j], dims, preferred_element_type=F32)
        out[order[8 + j], :n] = back.astype(BF16)
        out[order[8 + j], n:] = note


def project(order, hidden, own, other, teacher):
    size, width = own[0].shape
    rows = teacher.shape[0]
    anywhere = pl.BlockSpec(memory_space=pl.ANY)
    inside = pl.BlockSpec(memory_space=pltpu.VMEM)
    return pl.pallas_call(
        project_kernel,
        in_specs=[pl.BlockSpec(memory_space=pltpu.SMEM)] + [anywhere] * 16 + [inside],
        out_specs=inside,
        scratch_shapes=[
            pltpu.VMEM((8, rows, size), BF16),
            pltpu.VMEM((2, 8, size, width), BF16),
            pltpu.VMEM((2, rows, width), F32),
            pltpu.VMEM((2, rows, width), BF16),
            pltpu.SemaphoreType.DMA((6,)),
            pltpu.SemaphoreType.DMA((2, 8, 2)),
        ],
        out_shape=jax.ShapeDtypeStruct((8, rows + NOTE, size), BF16),
        compiler_params=pltpu.CompilerParams(vmem_limit_bytes=32 * 1024 * 1024),
        cost_estimate=pl.CostEstimate(
            flops=64 * rows * size * width, bytes_accessed=32 * size * width, transcendentals=0
        ),
    )(order, *hidden, *own, *other, teacher)


def teach_kernel(role, tokens, weight, out, away):
    product = jnp.dot(tokens[...], weight[...], preferred_element_type=F32)
    count, rows, width = out.shape
    first = role[0] == 0
    for i in range(count):
        low, high = product[:rows, i * width : (i + 1) * width], product[rows:, i * width : (i + 1) * width]
        out[i] = jnp.where(first, low, high).astype(BF16)
        away[i] = jnp.where(first, high, low).astype(BF16)


def teach(role, teacher_in, weight, blocks, width):
    _, rows, depth = teacher_in.shape
    shape = (blocks, rows, 2 * width)
    count = 4
    steps = blocks // count
    place = pl.BlockSpec((count, rows, width), lambda j, role: (j % steps, 0, j // steps))
    return pl.pallas_call(
        teach_kernel,
        grid_spec=pltpu.PrefetchScalarGridSpec(
            num_scalar_prefetch=1,
            grid=(2 * steps,),
            in_specs=[
                pl.BlockSpec((2 * rows, depth), lambda j, role: (0, 0)),
                pl.BlockSpec((depth, count * width), lambda j, role: (0, j)),
            ],
            out_specs=[place, place],
        ),
        out_shape=[jax.ShapeDtypeStruct(shape, BF16)] * 2,
        compiler_params=pltpu.CompilerParams(
            dimension_semantics=("arbitrary",), vmem_limit_bytes=40 * 1024 * 1024
        ),
        cost_estimate=pl.CostEstimate(
            flops=8 * rows * depth * blocks * width, bytes_accessed=4 * depth * blocks * width, transcendentals=0
        ),
    )(role, teacher_in.reshape(2 * rows, depth), weight)


def shards(teacher_in, teacher_weight, student_in, student_weight, projector):
    role = lax.axis_index("role")
    n_tensor = lax.axis_size("tensor")
    n_data = lax.axis_size("dp")
    own_rows = student_in.shape[0]
    total_rows = 2 * own_rows * n_data
    out_width = teacher_weight.shape[1]
    feat, hid = student_weight.shape
    wide = feat * n_data
    cols = projector.shape[1]

    xh = lax.axis_index("tensor") & 1

    w_first = gather_start(student_weight, "dp")

    swap = []
    for d in range(8):
        for t in range(8):
            to = ((t // 2 - d // 2) % 4) * 2 + (t ^ d) % 2
            swap.append((d * 8 + t, to * 8 + d))
    projector = lax.ppermute(projector, ("dp", "tensor"), swap)

    mine = lax.dynamic_slice_in_dim(student_in, role * wide, wide, axis=1)
    theirs = lax.dynamic_slice_in_dim(student_in, (1 - role) * wide, wide, axis=1)
    mine, theirs = lax.optimization_barrier((mine, theirs))
    theirs = flip(theirs)

    own, away = teach(jnp.full((1,), role, jnp.int32), teacher_in, teacher_weight, n_tensor, cols)
    away, projector, theirs, *w_first = lax.optimization_barrier((away, projector, theirs, *w_first))
    away = flip(away)

    up, down = ring_operands(student_weight, w_first)
    w_middle = [shift(up, "dp", 1, 0), shift(down, "dp", -1, 0)]
    p_other = shift(projector, "dp", 0, 1)

    zt = lax.axis_index("tensor") >> 1

    def teacher_part(k, first, count):
        at = ((zt - k) & 3) * 2 + first
        parts = (lax.dynamic_slice_in_dim(x, at, count, axis=0).astype(F32) for x in (own, away))
        return sum(parts)

    over = [teacher_part(2, e, 1).astype(BF16) for e in (0, 1)]
    *over, own, away = lax.optimization_barrier((*over, own, away))
    over = [shift(over[0], "tensor", -1, 0), shift(over[1], "tensor", 1, 0)]
    teacher = {k: teacher_part(k, 0, 2) for k in (0, 1, -1)}

    part = feat // 2
    at = sources("dp")
    student = jnp.concatenate([mine, theirs], axis=0)
    pre = sum(
        dot(lax.dynamic_slice_in_dim(student, at[j] * feat, feat, axis=1), block)
        for j, block in enumerate((student_weight, *w_first))
    )
    projector, p_other, pre, *moved = lax.optimization_barrier((projector, p_other, pre, *over, *w_middle))
    over, w_middle = moved[:2], moved[2:]
    teacher[1] = (teacher[1] + jnp.pad(over[0].astype(F32), ((0, 1), (0, 0), (0, 0)))).astype(BF16)
    teacher[-1] = (teacher[-1] + jnp.pad(over[1].astype(F32), ((1, 0), (0, 0), (0, 0)))).astype(BF16)
    teacher[1], teacher[-1], student_weight = lax.optimization_barrier((teacher[1], teacher[-1], student_weight))
    for k in (1, -1):
        teacher[k] = shift(teacher[k], "tensor", -k, 0)
    up, down = w_middle
    w_far = shift(jnp.concatenate([up[feat:], down[feat:]], axis=0), "dp", 0, 1)
    p_first = [shift(projector, "dp", 1, 0), shift(projector, "dp", -1, 0)]
    w_far, *p_first = lax.optimization_barrier((w_far, *p_first))
    p_first = [p_other, *p_first]

    def block_product(j, block):
        return dot(lax.dynamic_slice_in_dim(student, at[j] * feat, feat, axis=1), block)

    columns = lax.dynamic_slice_in_dim(student, at[4] * feat, feat, axis=1)
    pre = pre + block_product(5, up[:feat]) + block_product(6, down[:feat])
    pre = pre + dot(columns[:, :part], up[feat:]) + dot(columns[:, part:], down[feat:])
    pre = pre + block_product(7, w_far)
    pre = pre[:own_rows] + flip(pre[own_rows:])
    sigma = jax.nn.sigmoid(pre)
    hidden = (pre * sigma).astype(BF16)

    p_middle = gather_middle(projector, p_first, "dp")
    h_other = shift(hidden, "tensor", 0, 1)
    h_other, up, down, teacher[1], teacher[-1] = lax.optimization_barrier(
        (h_other, *p_middle, teacher[1], teacher[-1])
    )
    p_flip = flip(jnp.concatenate([after(projector, h_other), *p_first], axis=0))
    near = teacher[0] + teacher[1].astype(F32) + teacher[-1].astype(F32)
    cross = lax.dynamic_index_in_dim(near, 1 - xh, 0, False).astype(BF16)
    cross = shift(cross, "tensor", 0, 1)
    h_pair = jnp.concatenate([hidden, h_other], axis=0)
    h_before, h_after = shift(h_pair, "tensor", 1, 0), shift(h_pair, "tensor", -1, 0)
    p_far = [shift(up[:part], "dp", 1, 0), shift(down[part:feat], "dp", -1, 0)]
    h_before, h_after, cross, *p_far = lax.optimization_barrier((h_before, h_after, cross, *p_far))
    far_0 = shift(h_before[:own_rows], "tensor", 1, 0)
    far_1 = shift(h_after[own_rows:], "tensor", -1, 0)
    p_own = [projector, *p_first, up, down, *p_far]
    p_flip = [p_flip, flip(jnp.concatenate([up, down, *p_far], axis=0))]
    teacher = lax.dynamic_index_in_dim(near, xh, 0, False) + cross.astype(F32)
    hidden = [x.reshape(-1, own_rows, hid) for x in (hidden, h_other, h_after, far_0, far_1, h_before)]

    blocks = [((((zt + (d >> 1)) & 3) << 1) | ((d & 1) ^ xh)) for d in at]
    order = sources("dp") + blocks + [role]
    order = jnp.stack([jnp.asarray(x, jnp.int32) for x in order])
    back = project(order, hidden, p_own, p_flip, teacher)
    back = lax.all_to_all(back, "tensor", 0, 0, tiled=True)
    back = jnp.sum(back.astype(F32), axis=0)
    square = join_note(back[own_rows:])
    back = back[:own_rows]

    delta = (back * sigma * (1.0 + pre * (1.0 - sigma))).astype(BF16)
    packed = flip(jnp.concatenate([delta, split_note(square, hid)], axis=0))
    delta = jnp.concatenate([delta, packed[:own_rows]], axis=0)
    square = square + join_note(packed[own_rows:])

    grad = dot(student, delta, ((0,), (0,))).astype(BF16).reshape(n_data, feat, hid)
    note = jnp.broadcast_to(split_note(square, hid)[None], (n_data, NOTE, hid))
    grad = jnp.concatenate([grad, note], axis=1)
    grad = lax.all_to_all(grad, "dp", 0, 0, tiled=True)
    grad = jnp.sum(grad.astype(F32), axis=0)
    loss = join_note(grad[feat:])[0, 0] / (2.0 * total_rows * out_width)
    return (grad[:feat] / jnp.sqrt(jnp.float32(total_rows)), loss)


def solution(mesh):
    in_specs = (
        P(None, "dp", ("role", "tensor")),
        P(("role", "tensor"), None),
        P(("role", "dp"), None),
        P(("role", "dp"), "tensor"),
        P("tensor", ("role", "dp")),
    )
    out_specs = (P(("role", "dp"), "tensor"), P())
    return jax.shard_map(shards, mesh=mesh, in_specs=in_specs, out_specs=out_specs, check_vma=False)
```

```python
import jax
import jax.numpy as jnp
from jax import lax
from jax.experimental import pallas as pl
from jax.experimental.pallas import tpu as pltpu
from jax.sharding import PartitionSpec as P

BF16 = jnp.bfloat16
F32 = jnp.float32
NOTE = 16
OFFSETS = ((0, 0), (0, 1), (1, 0), (-1, 0), (2, 0), (1, 1), (-1, 1), (2, 1))


def shift(value, axis, k, e):
    perm = [(i, ((i // 2 + k) % 4) * 2 + ((i % 2) ^ e)) for i in range(8)]
    return lax.ppermute(value, axis, perm)


def flip(value):
    return lax.ppermute(value, "role", [(0, 1), (1, 0)])


def sources(axis):
    me = lax.axis_index(axis)
    return [((((me >> 1) - k) & 3) << 1) | ((me & 1) ^ e) for k, e in OFFSETS]


def after(value, *others):
    return lax.optimization_barrier((value, *others))[0]


def gather_start(block, axis):
    return [shift(block, axis, 0, 1), shift(block, axis, 1, 0), shift(block, axis, -1, 0)]


def ring_operands(block, first):
    other, before, nxt = first
    half = block.shape[0] // 2
    return jnp.concatenate([other, before[:half]], axis=0), jnp.concatenate([other, nxt[half:]], axis=0)


def gather_middle(block, first, axis):
    up, down = ring_operands(block, first)
    return [shift(up, axis, 1, 0), shift(down, axis, -1, 0)]


def dot(a, b, dims=((1,), (0,))):
    return lax.dot_general(a, b, (dims, ((), ())), preferred_element_type=F32)


def split_note(value, width):
    value = jnp.broadcast_to(value, (1, width)).astype(F32)
    row = lax.broadcasted_iota(jnp.int32, (NOTE, width), 0)
    high = lax.reduce_precision(value, 8, 7)
    middle = lax.reduce_precision(value - high, 8, 7)
    low = value - high - middle
    note = jnp.where(row == 0, high, jnp.where(row == 1, middle, jnp.where(row == 2, low, 0.0)))
    return note.astype(BF16)


def join_note(note):
    return jnp.sum(note.astype(F32), axis=0, keepdims=True)


def project_kernel(order, *refs):
    h_refs, own_refs, other_refs = refs[:6], refs[6:14], refs[14:16]
    teacher, out, h_kept, p_kept, total, residual, h_sem, p_sem = refs[16:]
    n, width = out.shape[1] - NOTE, out.shape[2]
    size = p_kept.shape[2]
    half = size // 2
    lengths = [size] * 4 + [size + half] * 2 + [half] * 2
    starts = [0, size, 2 * size, 3 * size, 0, size + half, 2 * (size + half), 3 * size + half]
    other_refs = [
        other_refs[i // 4].at[pl.ds(at, length)] for i, (at, length) in enumerate(zip(starts, lengths))
    ]
    h_copies = []
    for i, (ref, at, count) in enumerate(zip(h_refs, (0, 1, 2, 4, 5, 6), (1, 1, 2, 1, 1, 2))):
        h_copies.append(pltpu.make_async_copy(ref, h_kept.at[pl.ds(at, count)], h_sem.at[i]))
    for copy in h_copies:
        copy.start()
    low, high = pl.ds(0, half), pl.ds(half, half)

    def pieces(parts):
        block, other, before, nxt, up, down, *far = parts
        for whole in (block, other, before, nxt):
            yield whole.at[low], whole.at[high]
        yield up.at[pl.ds(size, half)], down.at[pl.ds(size, half)]
        for whole in (up, down):
            yield whole.at[low], whole.at[high]
        yield far[0].at[low], far[1].at[low]

    for j, sources_ in enumerate(zip(pieces(own_refs), pieces(other_refs))):
        for side, halves in enumerate(sources_):
            for part, source in enumerate(halves):
                target = p_kept.at[side, j, pl.ds(part * half, half)]
                pltpu.make_async_copy(source, target, p_sem.at[side, j, part]).start()

    first = order[16] == 0
    t_low, t_high = teacher[:, :width], teacher[:, width:]
    total[0] = -jnp.where(first, t_low, t_high)
    total[1] = -jnp.where(first, t_high, t_low)
    for copy in h_copies:
        copy.wait()

    @pl.loop(0, 4)
    def _(i):
        h = jnp.concatenate([h_kept[order[2 * i]], h_kept[order[2 * i + 1]]], axis=1)
        for side in range(2):
            for j in (2 * i, 2 * i + 1):
                for part in range(2):
                    target = p_kept.at[side, j, pl.ds(part * half, half)]
                    pltpu.make_async_copy(target, target, p_sem.at[side, j, part]).wait()
            block = p_kept[side, pl.ds(2 * i, 2)].reshape(2 * size, width)
            total[side] += jnp.dot(h, block, preferred_element_type=F32)

    squares = total[0] * total[0] + total[1] * total[1]
    value = jnp.broadcast_to(jnp.sum(squares, keepdims=True), (1, width))
    residual[...] = total[...].astype(BF16)
    row = lax.broadcasted_iota(jnp.int32, (NOTE, width), 0)
    top = value.astype(BF16).astype(F32)
    middle = (value - top).astype(BF16).astype(F32)
    bottom = value - top - middle
    note = jnp.where(row == 0, top, jnp.where(row == 1, middle, jnp.where(row == 2, bottom, 0.0)))
    note = note.astype(BF16)

    @pl.loop(0, 8)
    def _(j):
        dims = (((1,), (1,)), ((), ()))
        back = lax.dot_general(residual[0], p_kept[0, j], dims, preferred_element_type=F32)
        back += lax.dot_general(residual[1], p_kept[1, j], dims, preferred_element_type=F32)
        out[order[8 + j], :n] = back.astype(BF16)
        out[order[8 + j], n:] = note


def project(order, hidden, own, other, teacher):
    size, width = own[0].shape
    rows = teacher.shape[0]
    anywhere = pl.BlockSpec(memory_space=pl.ANY)
    inside = pl.BlockSpec(memory_space=pltpu.VMEM)
    return pl.pallas_call(
        project_kernel,
        in_specs=[pl.BlockSpec(memory_space=pltpu.SMEM)] + [anywhere] * 16 + [inside],
        out_specs=inside,
        scratch_shapes=[
            pltpu.VMEM((8, rows, size), BF16),
            pltpu.VMEM((2, 8, size, width), BF16),
            pltpu.VMEM((2, rows, width), F32),
            pltpu.VMEM((2, rows, width), BF16),
            pltpu.SemaphoreType.DMA((6,)),
            pltpu.SemaphoreType.DMA((2, 8, 2)),
        ],
        out_shape=jax.ShapeDtypeStruct((8, rows + NOTE, size), BF16),
        compiler_params=pltpu.CompilerParams(vmem_limit_bytes=32 * 1024 * 1024),
        cost_estimate=pl.CostEstimate(
            flops=64 * rows * size * width, bytes_accessed=32 * size * width, transcendentals=0
        ),
    )(order, *hidden, *own, *other, teacher)


def teach_kernel(role, tokens, weight, out, away):
    product = jnp.dot(tokens[...], weight[...], preferred_element_type=F32)
    count, rows, width = out.shape
    first = role[0] == 0
    for i in range(count):
        low, high = product[:rows, i * width : (i + 1) * width], product[rows:, i * width : (i + 1) * width]
        out[i] = jnp.where(first, low, high).astype(BF16)
        away[i] = jnp.where(first, high, low).astype(BF16)


def teach(role, teacher_in, weight, blocks, width):
    _, rows, depth = teacher_in.shape
    shape = (blocks, rows, 2 * width)
    count = 4
    steps = blocks // count
    place = pl.BlockSpec((count, rows, width), lambda j, role: (j % steps, 0, j // steps))
    return pl.pallas_call(
        teach_kernel,
        grid_spec=pltpu.PrefetchScalarGridSpec(
            num_scalar_prefetch=1,
            grid=(2 * steps,),
            in_specs=[
                pl.BlockSpec((2 * rows, depth), lambda j, role: (0, 0)),
                pl.BlockSpec((depth, count * width), lambda j, role: (0, j)),
            ],
            out_specs=[place, place],
        ),
        out_shape=[jax.ShapeDtypeStruct(shape, BF16)] * 2,
        compiler_params=pltpu.CompilerParams(
            dimension_semantics=("arbitrary",), vmem_limit_bytes=40 * 1024 * 1024
        ),
        cost_estimate=pl.CostEstimate(
            flops=8 * rows * depth * blocks * width, bytes_accessed=4 * depth * blocks * width, transcendentals=0
        ),
    )(role, teacher_in.reshape(2 * rows, depth), weight)


def shards(teacher_in, teacher_weight, student_in, student_weight, projector):
    role = lax.axis_index("role")
    n_tensor = lax.axis_size("tensor")
    n_data = lax.axis_size("dp")
    own_rows = student_in.shape[0]
    total_rows = 2 * own_rows * n_data
    out_width = teacher_weight.shape[1]
    feat, hid = student_weight.shape
    wide = feat * n_data
    cols = projector.shape[1]

    xh = lax.axis_index("tensor") & 1

    w_first = gather_start(student_weight, "dp")

    swap = []
    for d in range(8):
        for t in range(8):
            to = ((t // 2 - d // 2) % 4) * 2 + (t ^ d) % 2
            swap.append((d * 8 + t, to * 8 + d))
    projector = lax.ppermute(projector, ("dp", "tensor"), swap)

    mine = lax.dynamic_slice_in_dim(student_in, role * wide, wide, axis=1)
    theirs = lax.dynamic_slice_in_dim(student_in, (1 - role) * wide, wide, axis=1)
    mine, theirs = lax.optimization_barrier((mine, theirs))
    theirs = flip(theirs)

    own, away = teach(jnp.full((1,), role, jnp.int32), teacher_in, teacher_weight, n_tensor, cols)
    away, projector, theirs, *w_first = lax.optimization_barrier((away, projector, theirs, *w_first))
    away = flip(away)

    up, down = ring_operands(student_weight, w_first)
    w_middle = [shift(up, "dp", 1, 0), shift(down, "dp", -1, 0)]
    p_other = shift(projector, "dp", 0, 1)

    zt = lax.axis_index("tensor") >> 1

    def teacher_part(k, first, count):
        at = ((zt - k) & 3) * 2 + first
        parts = (lax.dynamic_slice_in_dim(x, at, count, axis=0).astype(F32) for x in (own, away))
        return sum(parts)

    over = [teacher_part(2, e, 1).astype(BF16) for e in (0, 1)]
    *over, own, away = lax.optimization_barrier((*over, own, away))
    over = [shift(over[0], "tensor", -1, 0), shift(over[1], "tensor", 1, 0)]
    teacher = {k: teacher_part(k, 0, 2) for k in (0, 1, -1)}

    part = feat // 2
    at = sources("dp")
    student = jnp.concatenate([mine, theirs], axis=0)
    pre = sum(
        dot(lax.dynamic_slice_in_dim(student, at[j] * feat, feat, axis=1), block)
        for j, block in enumerate((student_weight, *w_first))
    )
    projector, p_other, pre, *moved = lax.optimization_barrier((projector, p_other, pre, *over, *w_middle))
    over, w_middle = moved[:2], moved[2:]
    teacher[1] = (teacher[1] + jnp.pad(over[0].astype(F32), ((0, 1), (0, 0), (0, 0)))).astype(BF16)
    teacher[-1] = (teacher[-1] + jnp.pad(over[1].astype(F32), ((1, 0), (0, 0), (0, 0)))).astype(BF16)
    teacher[1], teacher[-1], student_weight = lax.optimization_barrier((teacher[1], teacher[-1], student_weight))
    for k in (1, -1):
        teacher[k] = shift(teacher[k], "tensor", -k, 0)
    up, down = w_middle
    w_far = shift(jnp.concatenate([up[feat:], down[feat:]], axis=0), "dp", 0, 1)
    p_first = [shift(projector, "dp", 1, 0), shift(projector, "dp", -1, 0)]
    w_far, *p_first = lax.optimization_barrier((w_far, *p_first))
    p_first = [p_other, *p_first]

    def block_product(j, block):
        return dot(lax.dynamic_slice_in_dim(student, at[j] * feat, feat, axis=1), block)

    columns = lax.dynamic_slice_in_dim(student, at[4] * feat, feat, axis=1)
    pre = pre + block_product(5, up[:feat]) + block_product(6, down[:feat])
    pre = pre + dot(columns[:, :part], up[feat:]) + dot(columns[:, part:], down[feat:])
    pre = pre + block_product(7, w_far)
    pre = pre[:own_rows] + flip(pre[own_rows:])
    sigma = jax.nn.sigmoid(pre)
    hidden = (pre * sigma).astype(BF16)

    p_middle = gather_middle(projector, p_first, "dp")
    h_other = shift(hidden, "tensor", 0, 1)
    h_other, up, down, teacher[1], teacher[-1] = lax.optimization_barrier(
        (h_other, *p_middle, teacher[1], teacher[-1])
    )
    p_flip = flip(jnp.concatenate([after(projector, h_other), *p_first], axis=0))
    near = teacher[0] + teacher[1].astype(F32) + teacher[-1].astype(F32)
    cross = lax.dynamic_index_in_dim(near, 1 - xh, 0, False).astype(BF16)
    cross = shift(cross, "tensor", 0, 1)
    h_pair = jnp.concatenate([hidden, h_other], axis=0)
    h_before, h_after = shift(h_pair, "tensor", 1, 0), shift(h_pair, "tensor", -1, 0)
    p_far = [shift(up[:part], "dp", 1, 0), shift(down[part:feat], "dp", -1, 0)]
    h_before, h_after, cross, *p_far = lax.optimization_barrier((h_before, h_after, cross, *p_far))
    far_0 = shift(h_before[:own_rows], "tensor", 1, 0)
    far_1 = shift(h_after[own_rows:], "tensor", -1, 0)
    p_own = [projector, *p_first, up, down, *p_far]
    p_flip = [p_flip, flip(jnp.concatenate([up, down, *p_far], axis=0))]
    teacher = lax.dynamic_index_in_dim(near, xh, 0, False) + cross.astype(F32)
    hidden = [x.reshape(-1, own_rows, hid) for x in (hidden, h_other, h_after, far_0, far_1, h_before)]

    blocks = [((((zt + (d >> 1)) & 3) << 1) | ((d & 1) ^ xh)) for d in at]
    order = sources("dp") + blocks + [role]
    order = jnp.stack([jnp.asarray(x, jnp.int32) for x in order])
    back = project(order, hidden, p_own, p_flip, teacher)
    back = lax.all_to_all(back, "tensor", 0, 0, tiled=True)
    back = jnp.sum(back.astype(F32), axis=0)
    square = join_note(back[own_rows:])
    back = back[:own_rows]

    delta = (back * sigma * (1.0 + pre * (1.0 - sigma))).astype(BF16)
    packed = flip(jnp.concatenate([delta, split_note(square, hid)], axis=0))
    delta = jnp.concatenate([delta, packed[:own_rows]], axis=0)
    square = square + join_note(packed[own_rows:])

    grad = dot(student, delta, ((0,), (0,))).astype(BF16).reshape(n_data, feat, hid)
    note = jnp.broadcast_to(split_note(square, hid)[None], (n_data, NOTE, hid))
    grad = jnp.concatenate([grad, note], axis=1)
    grad = lax.all_to_all(grad, "dp", 0, 0, tiled=True)
    grad = jnp.sum(grad.astype(F32), axis=0)
    loss = join_note(grad[feat:])[0, 0] / (2.0 * total_rows * out_width)
    return (grad[:feat] / jnp.sqrt(jnp.float32(total_rows)), loss)


def solution(mesh):
    in_specs = (
        P(None, "dp", ("role", "tensor")),
        P(("role", "tensor"), None),
        P(("role", "dp"), None),
        P(("role", "dp"), "tensor"),
        P("tensor", ("role", "dp")),
    )
    out_specs = (P(("role", "dp"), "tensor"), P())
    return jax.shard_map(shards, mesh=mesh, in_specs=in_specs, out_specs=out_specs, check_vma=False)
```
